512 devices in a mesh: dp: 8 (over y, x_lo), fsdp: 64 (over x_hi, z, core).
Axes of the slice: x: 4 (x_hi: 2, x_lo: 2; x = x_hi * 2 + x_lo), y: 4, z: 16, core: 2. Of those that a mesh axis runs over, the one named last changes fastest.
Arguments:
- hidden_in: bfloat16 [2048, 8192], P('dp', 'fsdp'), may hold values from -4 to 4
- out_grad: bfloat16 [2048, 8192], P('dp', 'fsdp'), may hold values from -6 to 6
- snapshot_ids: int32 [8, 256], P('dp'), may hold values from 0 to 3, never falling along the last dimension, each value on 1 to 128 neighbouring positions
- norm_gain: bfloat16 [8192], P('fsdp'), may hold values from 0.5 to 1.5
- wq_codes: bfloat16 [8192, 8192], P(None, 'fsdp'), may hold values from -0.044194174 to 0.044194174
- wq_scales: bfloat16 [256, 8192], P(None, 'fsdp'), may hold values from 0.5 to 2
- wkv_codes: bfloat16 [8192, 2048], P(None, 'fsdp'), may hold values from -0.044194174 to 0.044194174
- wkv_scales: bfloat16 [256, 2048], P(None, 'fsdp'), may hold values from 0.5 to 2
- wo_codes: bfloat16 [8192, 8192], P('fsdp'), may hold values from -0.0625 to 0.0625
- wo_scales: bfloat16 [256, 8192], P('fsdp'), may hold values from 0.5 to 2
- a_query: bfloat16 [64, 8192], P(None, 'fsdp'), may hold values from -0.0625 to 0.0625
- query_up_weight: bfloat16 [64, 8192], P(None, 'fsdp'), may hold values from -0.75 to 0.75
- a_value: bfloat16 [64, 8192], P(None, 'fsdp'), may hold values from -0.0625 to 0.0625
- value_up_weight: bfloat16 [64, 1024], P(None, 'fsdp'), may hold values from -0.75 to 0.75
Outputs:
- grad_a_query: float32 [8192, 64], P('fsdp')
- query_up_gradient: float32 [64, 8192], P(None, 'fsdp')
- grad_a_value: float32 [8192, 64], P('fsdp')
- grad_b_value: float32 [64, 1024], P(None, 'fsdp')
The draws below stay inside these ranges and needn't reach their ends.
Inputs may be any that keep to these rules, and one draw needn't show every extreme that they name: `snapshot_ids`: snapshot numbers never fall along a row; each snapshot spans 1 to 128 positions, and one spans exactly 128.
All inputs are finite; a program needn't handle non-finite values.
Results may differ from the reference program's by a relative error of at most 0.017.
The reference program's roundings to bfloat16 on the way count: a program that leaves them out, or rounds other values in their place, can miss the bound.
Values may be sent and summed in bfloat16 or wider, within the bound.
No kernel may reach another device: no remote copies, remote signals or barrier semaphores. Data moves between devices by JAX's collectives and lax.ppermute only.
A program may use at most 64 MiB of HBM per device.

```python
import math
import jax
import jax.numpy as jnp
import numpy as np
from jax import lax

D = 8192
HEAD_SIZE = 128
GROUP = 8
R = 64
LEN = 256
HEADS = 64
KEY_VALUE_HEADS = 8
TOKEN_COUNT = 2048
N_DP = 8


def draw_wq_codes(key, part):
    key = jax.random.fold_in(key, 3)
    bound = 4.0 * D ** (-0.5)
    codes = jax.random.normal(key, (D, HEADS * HEAD_SIZE), jnp.float32) * D ** (-0.5)
    return jnp.clip(codes, -bound, bound).astype(jnp.bfloat16)


def draw_wkv_codes(key, part):
    key = jax.random.fold_in(key, 5)
    bound = 4.0 * D ** (-0.5)
    codes = jax.random.normal(key, (D, 2 * KEY_VALUE_HEADS * HEAD_SIZE), jnp.float32) * D ** (-0.5)
    return jnp.clip(codes, -bound, bound).astype(jnp.bfloat16)


def draw_hidden_in(key, part):
    key = jax.random.fold_in(key, 7)
    noise_key = jax.random.fold_in(key, 0)
    values_out = jax.random.normal(noise_key, (TOKEN_COUNT, D), jnp.float32)
    return jnp.clip(values_out, -4.0, 4.0).astype(jnp.bfloat16)


def levels(rng, shape, cuts, low, largest):
    def one(dim, blocks):
        heights = jax.random.uniform(jax.random.fold_in(jax.random.fold_in(rng, 6), dim), (blocks,), jnp.float32, low / len(cuts), largest / len(cuts))
        return jnp.repeat(jnp.exp(heights), shape[dim] // blocks).reshape((-1,) + (1,) * (len(shape) - dim - 1))

    level = one(*cuts[0])
    for cut in cuts[1:]:
        level = level * one(*cut)
    return level


def profile(number_of, total, limit, slope):
    loads = [(1 << 20) // math.isqrt(grade ** slope) + 1 for grade in range(2, number_of + 1)]
    surplus, counts = total - limit - (number_of - 1), [1] * (number_of - 1)
    while surplus > 0:
        movable = [i for i in range(number_of - 1) if counts[i] < limit]
        whole, budget = sum([loads[i] for i in movable]), surplus
        for i in movable:
            extra = min(limit - counts[i], max(1, budget * loads[i] // whole), surplus)
            counts[i] = counts[i] + extra
            surplus = surplus - extra
    return np.array([limit] + counts)


def uneven_parts(key, amount, total, reach, lean):
    if amount == 2:
        one = jax.random.randint(key, (), max(1, total - reach), min(reach, total - 1) + 1)
        return jnp.stack([one, total - one])
    sizes = jnp.asarray(profile(amount, total, reach, lean), jnp.int32)
    couples = (amount - 1) // 2
    source_of, taker = sizes[1:1 + 2 * couples:2], sizes[2:2 + 2 * couples:2]
    margin = jnp.minimum(source_of - 1, reach - taker)
    passed = jax.random.randint(jax.random.fold_in(key, 1), (couples,), 0, 1 << 20) % (margin + 1)
    sizes = sizes.at[1:1 + 2 * couples:2].set(source_of - passed).at[2:2 + 2 * couples:2].set(taker + passed)
    return sizes[jax.random.permutation(jax.random.fold_in(key, 2), amount)]


def noise(key, extent, scale, most, cuts=(), held_as=jnp.bfloat16):
    drawn = jax.random.normal(key, extent, jnp.float32) * scale
    if len(cuts) > 0:
        drawn = levels(key, extent, cuts, -0.22, 0.18) * drawn
    return jnp.clip(drawn, min=-most, max=most).astype(held_as)


def setup_inputs(seed: int = 0) -> dict:
    arg_keys = jax.random.split(jax.random.key(seed), 15)
    return {
        "hidden_in": draw_hidden_in(jax.random.fold_in(arg_keys[14], 71), 0),
        "out_grad": noise(arg_keys[1], (TOKEN_COUNT, D), 1.0, 6.0, ((0, 8), (1, 64))),
        "snapshot_ids": jax.vmap(lambda own: jnp.searchsorted(jnp.cumsum(uneven_parts(own, 4, LEN, LEN // 2, 0)), jnp.arange(LEN), side="right"))(jax.random.split(arg_keys[2], N_DP)).reshape((N_DP, LEN)).astype(jnp.int32),
        "norm_gain": jnp.clip(1.0 + 0.1 * jax.random.normal(arg_keys[3], (D,), jnp.float32), 0.5, 1.5).astype(jnp.bfloat16),
        "wq_codes": draw_wq_codes(jax.random.fold_in(arg_keys[14], 71), 0),
        "wq_scales": jnp.clip(jnp.exp(math.log(2.0) - 1.3862944 * jax.random.uniform(arg_keys[5], (D // 32, HEADS * HEAD_SIZE), jnp.float32) ** levels(arg_keys[5], (D // 32, HEADS * HEAD_SIZE), ((1, 64),), -0.2, 0.2)), 0.5, 2.0).astype(jnp.bfloat16),
        "wkv_codes": draw_wkv_codes(jax.random.fold_in(arg_keys[14], 71), 0),
        "wkv_scales": jnp.clip(jnp.exp(math.log(2.0) - 1.3862944 * jax.random.uniform(arg_keys[7], (D // 32, 2 * KEY_VALUE_HEADS * HEAD_SIZE), jnp.float32) ** levels(arg_keys[7], (D // 32, 2 * KEY_VALUE_HEADS * HEAD_SIZE), ((1, 64),), -0.2, 0.2)), 0.5, 2.0).astype(jnp.bfloat16),
        "wo_codes": noise(arg_keys[8], (HEADS * HEAD_SIZE, D), (HEADS * HEAD_SIZE) ** -0.5, 0.0625, ((0, 64),)),
        "wo_scales": jnp.clip(jnp.exp(math.log(2.0) - 1.3862944 * jax.random.uniform(arg_keys[9], (HEADS * HEAD_SIZE // 32, D), jnp.float32) ** levels(arg_keys[9], (HEADS * HEAD_SIZE // 32, D), ((0, 64),), -0.2, 0.2)), 0.5, 2.0).astype(jnp.bfloat16),
        "a_query": noise(arg_keys[10], (R, D), D ** -0.5, 0.0625, ((1, 64),)),
        "query_up_weight": noise(arg_keys[11], (R, HEADS * HEAD_SIZE), R ** -0.5, 0.75, ((1, 64),)),
        "a_value": noise(arg_keys[12], (R, D), D ** -0.5, 0.0625, ((1, 64),)),
        "value_up_weight": noise(arg_keys[13], (R, KEY_VALUE_HEADS * HEAD_SIZE), R ** -0.5, 0.75, ((1, 64),)),
    }


EPS = 1e-05
ADAPTER_SCALE = 0.5
ROPE_BASE = 500000.0
MASKED = -1e+30

def dequantize(codes, scales, block_axis):
    block_rows = codes.shape[block_axis] // scales.shape[block_axis]
    scale_wide = jnp.repeat(scales.astype(jnp.float32), block_rows, axis=block_axis)
    return (codes.astype(jnp.float32) * scale_wide).astype(jnp.bfloat16)

def rope_tables(length, head_dim):
    half_width = head_dim // 2
    positions = jnp.arange(length).astype(jnp.float32)[:, None]
    frequency = jnp.exp(jnp.arange(half_width).astype(jnp.float32) * (-2.0 * math.log(ROPE_BASE) / head_dim))
    angles = positions * frequency[None, :]
    return (jnp.cos(angles), jnp.sin(angles))

def rotate(values_in, cosine_table, sine_table):
    half_width = values_in.shape[-1] // 2
    front_half = values_in[..., :half_width]
    back_half = values_in[..., half_width:]
    return jnp.concatenate([front_half * cosine_table - back_half * sine_table, back_half * cosine_table + front_half * sine_table], axis=-1)

def unrotate(grads_in, cosine_table, sine_table):
    half_width = grads_in.shape[-1] // 2
    front_half = grads_in[..., :half_width]
    back_half = grads_in[..., half_width:]
    return jnp.concatenate([front_half * cosine_table + back_half * sine_table, back_half * cosine_table - front_half * sine_table], axis=-1)

def reference(hidden_in, out_grad, snapshot_ids, norm_gain, wq_codes, wq_scales, wkv_codes, wkv_scales, wo_codes, wo_scales, a_query, query_up_weight, a_value, value_up_weight):
    hidden_f = hidden_in.astype(jnp.float32)
    mean_sq = lax.optimization_barrier(jnp.mean(hidden_f * hidden_f, axis=1, keepdims=True))
    normalized_input = (hidden_f * lax.rsqrt(mean_sq + EPS) * norm_gain.astype(jnp.float32)[None, :]).astype(jnp.bfloat16)
    query_weight_full = dequantize(wq_codes, wq_scales, 0)
    wkv_full = dequantize(wkv_codes, wkv_scales, 0)
    wo_full = dequantize(wo_codes, wo_scales, 0)
    query_rank_rows = jnp.dot(normalized_input, a_query.T, preferred_element_type=jnp.float32).astype(jnp.bfloat16)
    value_rank_rows = jnp.dot(normalized_input, a_value.T, preferred_element_type=jnp.float32).astype(jnp.bfloat16)
    query_linear = jnp.dot(normalized_input, query_weight_full, preferred_element_type=jnp.float32) + ADAPTER_SCALE * jnp.dot(query_rank_rows, query_up_weight, preferred_element_type=jnp.float32)
    key_value_linear = jnp.dot(normalized_input, wkv_full, preferred_element_type=jnp.float32).reshape(TOKEN_COUNT, KEY_VALUE_HEADS, 2, HEAD_SIZE)
    value_adapter = ADAPTER_SCALE * jnp.dot(value_rank_rows, value_up_weight, preferred_element_type=jnp.float32)
    key_value_linear = key_value_linear.at[:, :, 1, :].add(value_adapter.reshape(TOKEN_COUNT, KEY_VALUE_HEADS, HEAD_SIZE))
    kv_round = key_value_linear.astype(jnp.bfloat16)
    cosine_table, sine_table = rope_tables(LEN, HEAD_SIZE)
    cosine_four = cosine_table[None, :, None, :]
    sine_four = sine_table[None, :, None, :]
    queries = rotate(query_linear.reshape(N_DP, LEN, HEADS, HEAD_SIZE), cosine_four, sine_four).astype(jnp.bfloat16)
    keys_rot = rotate(kv_round[:, :, 0, :].astype(jnp.float32).reshape(N_DP, LEN, KEY_VALUE_HEADS, HEAD_SIZE), cosine_four, sine_four).astype(jnp.bfloat16)
    values_grp = kv_round[:, :, 1, :].reshape(N_DP, LEN, KEY_VALUE_HEADS, HEAD_SIZE)
    keys_head = jnp.repeat(keys_rot, GROUP, axis=2).astype(jnp.float32)
    values_head = jnp.repeat(values_grp, GROUP, axis=2).astype(jnp.float32)
    score_scale = HEAD_SIZE ** (-0.5)
    scores = jnp.einsum('bqhd,bkhd->bhqk', queries.astype(jnp.float32), keys_head) * score_scale
    positions = jnp.arange(LEN)
    causal = positions[None, :] <= positions[:, None]
    same_snap = snapshot_ids[:, :, None] == snapshot_ids[:, None, :]
    allowed = jnp.logical_and(causal[None, :, :], same_snap)[:, None, :, :]
    scores = jnp.where(allowed, scores, MASKED)
    row_top = lax.optimization_barrier(jnp.max(scores, axis=-1, keepdims=True))
    weights_raw = jnp.exp(scores - row_top)
    prob = weights_raw / lax.optimization_barrier(jnp.sum(weights_raw, axis=-1, keepdims=True))
    prob_b = prob.astype(jnp.bfloat16)
    grad_ctx = jnp.dot(out_grad, wo_full.T, preferred_element_type=jnp.float32).astype(jnp.bfloat16)
    grad_ctx = grad_ctx.reshape(N_DP, LEN, HEADS, HEAD_SIZE).astype(jnp.float32)
    grad_prob = jnp.einsum('bqhd,bkhd->bhqk', grad_ctx, values_head)
    value_gradient = jnp.einsum('bhqk,bqhd->bkhd', prob_b.astype(jnp.float32), grad_ctx).astype(jnp.bfloat16)
    grad_score = (prob * (grad_prob - lax.optimization_barrier(jnp.sum(prob * grad_prob, axis=-1, keepdims=True)))).astype(jnp.bfloat16)
    grad_query = jnp.einsum('bhqk,bkhd->bqhd', grad_score.astype(jnp.float32), keys_head) * score_scale
    query_linear_gradient = unrotate(grad_query, cosine_four, sine_four).astype(jnp.bfloat16).reshape(TOKEN_COUNT, HEADS * HEAD_SIZE)
    value_gradient = value_gradient.reshape(TOKEN_COUNT, HEADS * HEAD_SIZE)
    query_up_gradient = ADAPTER_SCALE * jnp.dot(query_rank_rows.T, query_linear_gradient, preferred_element_type=jnp.float32)
    value_per_head = ADAPTER_SCALE * jnp.dot(value_rank_rows.T, value_gradient, preferred_element_type=jnp.float32)
    grad_b_value = lax.optimization_barrier(jnp.sum(value_per_head.reshape(R, KEY_VALUE_HEADS, GROUP, HEAD_SIZE), axis=2)).reshape(R, KEY_VALUE_HEADS * HEAD_SIZE)
    value_up_per_head = jnp.repeat(value_up_weight.reshape(R, KEY_VALUE_HEADS, HEAD_SIZE), GROUP, axis=1).reshape(R, HEADS * HEAD_SIZE)
    query_rank_gradient = ADAPTER_SCALE * jnp.dot(query_linear_gradient, query_up_weight.T, preferred_element_type=jnp.float32)
    value_rank_gradient = ADAPTER_SCALE * jnp.dot(value_gradient, value_up_per_head.T, preferred_element_type=jnp.float32)
    normed_f = normalized_input.astype(jnp.float32)
    grad_a_query = jnp.dot(normed_f.T, query_rank_gradient, precision=lax.Precision.HIGHEST)
    grad_a_value = jnp.dot(normed_f.T, value_rank_gradient, precision=lax.Precision.HIGHEST)
    return (grad_a_query, query_up_gradient, grad_a_value, grad_b_value)
```

```python
import math

import jax
import jax.numpy as jnp
from jax import lax
from jax.sharding import PartitionSpec as P

GROUP = 8
EPS = 1e-05
ADAPTER_SCALE = 0.5
ROPE_BASE = 500000.0
MASKED = -1e30

NX, NZ, NC = 2, 16, 2
MASKS = (1, 32, 33)


def place(a, z, c):
    return a * (NZ * NC) + z * NC + c


Z_GROUPS = [[place(a, z, c) for z in range(NZ)] for a in range(NX) for c in range(NC)]
NEAR_GROUPS = [[GROUP * g + i for i in range(GROUP)] for g in range(8)]
FAR_GROUPS = [
    [place(a, z + 4 * k, c) for a in range(NX) for k in range(4)] for z in range(4) for c in range(NC)
]


def xor_pairs(mask):
    return [(i, i ^ mask) for i in range(NX * NZ * NC)]


def z_pairs(step):
    return [
        (place(a, z, c), place(a, (z + step) % NZ, c))
        for a in range(NX)
        for z in range(NZ)
        for c in range(NC)
    ]


def swap(value, mask):
    return lax.ppermute(value, "fsdp", xor_pairs(mask))


def rope_tables(length, head_dim):
    half_width = head_dim // 2
    positions = jnp.arange(length).astype(jnp.float32)[:, None]
    frequency = jnp.exp(
        jnp.arange(half_width).astype(jnp.float32) * (-2.0 * math.log(ROPE_BASE) / head_dim)
    )
    angles = positions * frequency[None, :]
    return (jnp.cos(angles), jnp.sin(angles))


def rotate(values_in, cosine_table, sine_table):
    half_width = values_in.shape[-1] // 2
    front_half = values_in[..., :half_width]
    back_half = values_in[..., half_width:]
    return jnp.concatenate(
        [
            front_half * cosine_table - back_half * sine_table,
            back_half * cosine_table + front_half * sine_table,
        ],
        axis=-1,
    )


def unrotate(grads_in, cosine_table, sine_table):
    return rotate(grads_in, cosine_table, -sine_table)


def contract(left_arr, right_arr, left_dim, right_dim):
    return lax.dot_general(
        left_arr,
        right_arr,
        (((left_dim,), (right_dim,)), ((), ())),
        preferred_element_type=jnp.float32,
    )


def two_terms(value):
    high = lax.reduce_precision(value, 8, 7)
    return high.astype(jnp.bfloat16), (value - high).astype(jnp.bfloat16)


def collect_group(own_columns, head_index):
    running = own_columns
    for level_bit in range(GROUP.bit_length() - 1):
        partner = swap(running, 1 << level_bit)
        upper_side = head_index // (1 << level_bit) % 2 == 1
        running = jnp.where(
            upper_side,
            jnp.concatenate([partner, running], axis=1),
            jnp.concatenate([running, partner], axis=1),
        )
    return running


def relative_order(blocks, z_index, axis):
    flipped = jnp.roll(jnp.flip(blocks, axis), 1, axis)
    doubled = jnp.concatenate([flipped, flipped], axis=axis)
    return lax.dynamic_slice_in_dim(doubled, (NZ - z_index) % NZ, NZ, axis)


def quarter(blocks, x_index, core_index, axis):
    taken = lax.dynamic_index_in_dim(blocks, x_index, axis, keepdims=False)
    return lax.dynamic_index_in_dim(taken, core_index, axis + 1, keepdims=False)


def spread(value, number):
    return jnp.broadcast_to(value[None], (number,) + value.shape)


def exchange(value, axis, groups=None):
    return lax.all_to_all(value, axis, 0, 0, axis_index_groups=groups)


def local(
    hidden_in,
    out_grad,
    snapshot_ids,
    norm_gain,
    wq_codes,
    wq_scales,
    wkv_codes,
    wkv_scales,
    wo_codes,
    wo_scales,
    a_query,
    query_up_weight,
    a_value,
    value_up_weight,
):
    f32, bf16 = jnp.float32, jnp.bfloat16
    head_index = lax.axis_index("fsdp")
    x_index = head_index // (NZ * NC)
    z_index = head_index // NC % NZ
    core_index = head_index % NC
    member = head_index % GROUP
    length, width = hidden_in.shape
    features = wq_codes.shape[0]
    rank = a_query.shape[0]
    kv_width = wkv_codes.shape[1]
    key_members = 128 // kv_width

    hidden_f = hidden_in.astype(f32)
    square_own = jnp.sum(hidden_f * hidden_f, axis=1)
    gained = (hidden_f * norm_gain.astype(f32)[None, :]).astype(bf16)
    square_high, square_low = two_terms(square_own)
    packet = jnp.concatenate(
        [
            gained,
            a_query,
            a_value,
            square_high.reshape(2, 128),
            square_low.reshape(2, 128),
            jnp.zeros((12, 128), bf16),
        ],
        axis=0,
    )
    dy_quarter = lax.all_gather(out_grad, "fsdp", axis=1, tiled=True, axis_index_groups=Z_GROUPS)

    forward, backward = [packet], [packet]
    for step in range(NZ // 2):
        forward.append(lax.ppermute(forward[-1], "fsdp", z_pairs(1)))
        if step < NZ // 2 - 1:
            backward.append(lax.ppermute(backward[-1], "fsdp", z_pairs(-1)))
    pieces = forward + backward[:0:-1]

    wq_blocks = wq_codes.reshape(NX, NZ, NC, 4, 32, 128)
    wq_levels = wq_scales.reshape(NX, NZ, NC, 4, 1, 128)
    wkv_blocks = wkv_codes.reshape(NX, NZ, NC, 4, 32, kv_width)
    wkv_levels = wkv_scales.reshape(NX, NZ, NC, 4, 1, kv_width)
    wo_blocks = wo_codes.reshape(4, 32, NX, NZ, NC, 128)
    wo_levels = wo_scales.reshape(4, 1, NX, NZ, NC, 128)

    def projection_of(mask):
        of_x, of_c = x_index ^ (mask // 32), core_index ^ (mask % 2)
        wq_part = (
            quarter(wq_blocks, of_x, of_c, 0).astype(f32) * quarter(wq_levels, of_x, of_c, 0).astype(f32)
        ).astype(bf16)
        wq_part = relative_order(wq_part.reshape(NZ, 128, 128), z_index, 0)
        wkv_part = (
            quarter(wkv_blocks, of_x, of_c, 0).astype(f32) * quarter(wkv_levels, of_x, of_c, 0).astype(f32)
        ).astype(bf16)
        wkv_part = jnp.transpose(wkv_part.reshape(NZ, 128, kv_width), (2, 0, 1))
        wkv_part = relative_order(wkv_part, z_index, 1)
        return jnp.concatenate(
            [wq_part.reshape(NZ * 128, 128), wkv_part.reshape(kv_width * NZ, 128)], axis=0
        )

    def output_of(mask):
        of_x, of_c = x_index ^ (mask // 32), core_index ^ (mask % 2)
        part = quarter(wo_blocks, of_x, of_c, 2).astype(f32) * quarter(wo_levels, of_x, of_c, 2).astype(f32)
        return part.astype(bf16).reshape(128, NZ * 128)

    projections = [projection_of(0)] + [swap(projection_of(mask), mask) for mask in MASKS]
    outputs = [output_of(0)] + [swap(output_of(mask), mask) for mask in MASKS]
    value_up_group = collect_group(value_up_weight, head_index)

    wq_all = jnp.concatenate([p[: NZ * 128] for p in projections], axis=1)
    wkv_all = jnp.concatenate([p[NZ * 128 :].reshape(kv_width, NZ * 128) for p in projections], axis=0)
    wo_all = jnp.concatenate(outputs, axis=0)

    inputs = jnp.concatenate([p[:length] for p in pieces], axis=1)
    downs = jnp.concatenate([p[length : length + 2 * rank] for p in pieces], axis=1)
    squares = sum(
        p[length + 2 * rank : length + 2 * rank + 2].astype(f32)
        + p[length + 2 * rank + 2 : length + 2 * rank + 4].astype(f32)
        for p in pieces
    )
    q_parts = contract(inputs, wq_all, 1, 0)
    kv_parts = contract(inputs, wkv_all, 1, 1)
    low_part = contract(inputs, downs, 1, 1)
    squares_high, squares_low = two_terms(squares)

    def parcel(slot):
        kv_part = kv_parts[:, slot * kv_width : (slot + 1) * kv_width]
        kv_part = jnp.concatenate([kv_part[64 * j : 64 * j + 64] for j in range(4)], axis=1)
        return jnp.concatenate(
            [
                q_parts[:, slot * 128 : (slot + 1) * 128].astype(bf16),
                low_part.astype(bf16),
                kv_part.astype(bf16),
                squares_high,
                squares_low,
                jnp.zeros((12, 128), bf16),
            ],
            axis=0,
        )

    arrived = [swap(parcel(slot + 1), mask) for slot, mask in enumerate(MASKS)]
    q_sum = q_parts[:, :128] + sum(p[:length].astype(f32) for p in arrived)
    low_sum = low_part + sum(p[length : 2 * length].astype(f32) for p in arrived)
    kv_own = kv_parts[:, :kv_width]
    kv_own = jnp.concatenate([kv_own[64 * j : 64 * j + 64] for j in range(4)], axis=1)
    kv_sum = kv_own + sum(p[2 * length : 2 * length + 64].astype(f32) for p in arrived)
    square_sum = squares + sum(
        p[2 * length + 64 : 2 * length + 66].astype(f32) + p[2 * length + 66 : 2 * length + 68].astype(f32)
        for p in arrived
    )
    inverse = lax.rsqrt(square_sum.reshape(length, 1) / features + EPS)
    low_both = (low_sum * inverse).astype(bf16)
    query_rank_rows, value_rank_rows = low_both[:, :rank], low_both[:, rank:]

    kv_columns = jnp.concatenate([kv_sum[:, 32 * j : 32 * j + 32] for j in range(4)], axis=0) * inverse
    adapter_columns = lax.dynamic_slice_in_dim(
        value_up_group, jnp.maximum(member - key_members, 0) * kv_width, kv_width, 1
    )
    adapter_contribution = ADAPTER_SCALE * contract(value_rank_rows, adapter_columns, 1, 0)
    kv_columns = (kv_columns + jnp.where(member >= key_members, adapter_contribution, 0.0)).astype(bf16)
    kv_group = exchange(spread(kv_columns.reshape(64, 128), GROUP), "fsdp", NEAR_GROUPS)
    kv_group = jnp.transpose(kv_group.reshape(GROUP, length, kv_width), (1, 0, 2)).reshape(length, -1)
    head_dim = 128
    query_linear = q_sum * inverse + ADAPTER_SCALE * contract(query_rank_rows, query_up_weight, 1, 0)

    cosine_table, sine_table = rope_tables(length, head_dim)
    queries = rotate(query_linear, cosine_table, sine_table).astype(bf16)
    keys_rot = rotate(kv_group[:, :head_dim].astype(f32), cosine_table, sine_table).astype(bf16)
    values_grp = kv_group[:, head_dim:]
    score_scale = head_dim ** (-0.5)
    scores = contract(queries, keys_rot, 1, 1) * score_scale
    positions = jnp.arange(length)
    causal = positions[None, :] <= positions[:, None]
    segment = snapshot_ids[0]
    allowed = jnp.logical_and(causal, segment[:, None] == segment[None, :])
    scores = jnp.where(allowed, scores, MASKED)
    row_top = jnp.max(scores, axis=-1, keepdims=True)
    weights_raw = jnp.exp(scores - row_top)
    prob = weights_raw / jnp.sum(weights_raw, axis=-1, keepdims=True)
    prob_b = prob.astype(bf16)

    ctx_parts = contract(dy_quarter, wo_all, 1, 1)
    ctx_arrived = [
        swap(ctx_parts[:, 128 * (slot + 1) : 128 * (slot + 2)].astype(bf16), mask)
        for slot, mask in enumerate(MASKS)
    ]
    grad_ctx = (ctx_parts[:, :128] + sum(p.astype(f32) for p in ctx_arrived)).astype(bf16)

    grad_prob = contract(grad_ctx, values_grp, 1, 1)
    value_gradient = contract(prob_b, grad_ctx, 0, 0).astype(bf16)
    grad_score = (prob * (grad_prob - jnp.sum(prob * grad_prob, axis=-1, keepdims=True))).astype(bf16)
    grad_query = contract(grad_score, keys_rot, 1, 0) * score_scale
    query_linear_gradient = unrotate(grad_query, cosine_table, sine_table).astype(bf16)
    query_up_output = ADAPTER_SCALE * contract(query_rank_rows, query_linear_gradient, 0, 0)
    value_contribution = ADAPTER_SCALE * contract(value_rank_rows, value_gradient, 0, 0)
    grad_low = jnp.concatenate(
        [
            ADAPTER_SCALE * contract(query_linear_gradient, query_up_weight, 1, 1),
            ADAPTER_SCALE * contract(value_gradient, value_up_group, 1, 1),
        ],
        axis=1,
    )

    slice_rows = length // GROUP
    own_width = head_dim // GROUP
    value_slices = jnp.transpose(value_contribution.reshape(rank, GROUP, own_width), (1, 0, 2))
    outgoing = jnp.concatenate(
        [
            grad_low.astype(bf16).reshape(GROUP, slice_rows, 128),
            value_slices.reshape(GROUP, 8, 128).astype(bf16),
        ],
        axis=1,
    )
    near = jnp.sum(exchange(outgoing, "fsdp", NEAR_GROUPS).astype(f32), axis=0)
    low_near, value_here = near[:slice_rows], near[slice_rows:]
    far = exchange(spread(low_near.astype(bf16), 8), "fsdp", FAR_GROUPS)
    low_slice = jnp.sum(far.astype(f32), axis=0).astype(bf16)
    low_total = exchange(spread(low_slice, GROUP), "fsdp", NEAR_GROUPS).reshape(length, 128)
    normalized = (hidden_f * inverse * norm_gain.astype(f32)[None, :]).astype(bf16)
    rows_here = contract(normalized, low_total, 0, 0)

    mine = jnp.concatenate([rows_here, query_up_output, value_here], axis=0).astype(bf16)
    total = jnp.sum(exchange(spread(mine, 8), "dp").astype(f32), axis=0)
    rows_total = total[:width]
    return (
        rows_total[:, :rank],
        total[width : width + rank],
        rows_total[:, rank:],
        total[width + rank :].reshape(rank, own_width),
    )


def solution(mesh):
    in_specs = (
        P("dp", "fsdp"),
        P("dp", "fsdp"),
        P("dp", None),
        P("fsdp"),
        P(None, "fsdp"),
        P(None, "fsdp"),
        P(None, "fsdp"),
        P(None, "fsdp"),
        P("fsdp", None),
        P("fsdp", None),
        P(None, "fsdp"),
        P(None, "fsdp"),
        P(None, "fsdp"),
        P(None, "fsdp"),
    )
    out_specs = (P("fsdp", None), P(None, "fsdp"), P("fsdp", None), P(None, "fsdp"))
    return jax.shard_map(local, mesh=mesh, in_specs=in_specs, out_specs=out_specs, check_vma=False)
```

```python
import math

import jax
import jax.numpy as jnp
import numpy as np
from jax import lax
from jax.experimental import pallas as pl
from jax.experimental.pallas import tpu as pltpu
from jax.sharding import PartitionSpec as P

GROUP = 8
EPS = 1e-05
ADAPTER_SCALE = 0.5
ROPE_BASE = 500000.0
MASKED = -1e30

NX, NZ, NC = 2, 16, 2
LENGTH, HEAD, RANK, KV = 256, 128, 64, 32
FEATURES = NX * NZ * NC * HEAD
STEPS = NZ // 2
BLOCKS = 2 * STEPS
PACKET = LENGTH + 2 * RANK + 16
PER_HEAD = 2 * LENGTH + 2 * KV
SHARED = LENGTH + 16

F32, BF16 = jnp.float32, jnp.bfloat16
VMEM = pl.BlockSpec(memory_space=pltpu.VMEM)
SMEM = pl.BlockSpec(memory_space=pltpu.SMEM)


def place(a, z, c):
    return a * (NZ * NC) + z * NC + c


NEAR_GROUPS = [[GROUP * g + i for i in range(GROUP)] for g in range(8)]
FAR_GROUPS = [
    [place(a, z + 4 * k, c) for a in range(NX) for k in range(4)] for z in range(4) for c in range(NC)
]
RING = [
    (place(a, z, c), place(a, (z + (1 if c == 0 else -1)) % NZ, c))
    for a in range(NX)
    for z in range(NZ)
    for c in range(NC)
]
LAST = [pair for pair in RING if pair[0] % NC == 1]
TO_MEMBER = [(GROUP * g + 2 * q + q % 2, GROUP * g + 4 + q) for g in range(8) for q in range(4)]


def swap(value, mask):
    return lax.ppermute(value, "fsdp", [(i, i ^ mask) for i in range(NX * NZ * NC)])


def exchange(value, axis, groups=None):
    return lax.all_to_all(value, axis, 0, 0, axis_index_groups=groups)


def after(value, *others):
    return lax.optimization_barrier((value, *others))[0]


def rope_tables():
    positions = np.arange(LENGTH, dtype=np.float32)[:, None]
    steps = np.arange(HEAD // 2, dtype=np.float32)
    frequency = np.exp(steps * np.float32(-2.0 * math.log(ROPE_BASE) / HEAD)).astype(np.float32)
    angles = positions * frequency[None, :]
    return np.cos(angles).astype(np.float32), np.sin(angles).astype(np.float32)


def contract(left_arr, right_arr, left_dim, right_dim):
    return lax.dot_general(
        left_arr,
        right_arr,
        (((left_dim,), (right_dim,)), ((), ())),
        preferred_element_type=F32,
    )


def two_terms(value):
    high = value.astype(BF16)
    return high, (value - high.astype(F32)).astype(BF16)


def call(body, outs, *operands, scratch=(), megabytes=32):
    specs = [SMEM if o.dtype == jnp.int32 and o.ndim == 1 else VMEM for o in operands]
    many = isinstance(outs, (list, tuple))
    return pl.pallas_call(
        body,
        out_shape=outs,
        in_specs=specs,
        out_specs=[VMEM] * len(outs) if many else VMEM,
        scratch_shapes=list(scratch),
        compiler_params=pltpu.CompilerParams(vmem_limit_bytes=megabytes << 20),
    )(*operands)


def shape(*dims, dtype=BF16):
    return jax.ShapeDtypeStruct(dims, dtype)


def diagonal(size):
    return lax.broadcasted_iota(jnp.int32, (size, size), 0) == lax.broadcasted_iota(
        jnp.int32, (size, size), 1
    )


def to_row(column):
    return jnp.sum(jnp.where(diagonal(128), column, 0.0), axis=0, keepdims=True)


def to_column(row):
    return jnp.sum(jnp.where(diagonal(128), row, 0.0), axis=1, keepdims=True)


def pack_kernel(hidden, gain, a_query, a_value, value_up, packet):
    values = hidden[...].astype(F32)
    packet[:LENGTH] = (values * gain[...].astype(F32)).astype(BF16)
    packet[LENGTH : LENGTH + RANK] = a_query[...]
    packet[LENGTH + RANK : LENGTH + 2 * RANK] = a_value[...]
    squares = jnp.sum(values * values, axis=1, keepdims=True)
    rows = jnp.concatenate([to_row(squares[:128]), to_row(squares[128:])], axis=0)
    high, low = two_terms(rows)
    base = LENGTH + 2 * RANK
    packet[base : base + 16] = jnp.concatenate([high, low, jnp.zeros((12, 128), BF16)], axis=0)
    columns = value_up[...].astype(F32).T
    columns = jnp.concatenate([columns, jnp.zeros((16, 128 - RANK), F32)], axis=1)
    packet[base + 16 : base + 32] = columns.astype(BF16)


def source_block(place_ref, slot, j):
    peer_x = place_ref[0] ^ (slot >> 1)
    peer_c = place_ref[2] ^ (slot & 1)
    hops = jnp.where(j < STEPS - 1, j + 1, peer_c * STEPS)
    z = (place_ref[1] + jnp.where(peer_c == 0, NZ - hops, hops)) % NZ
    return peer_x * (NZ * NC) + z * NC, peer_c


def projection_kernel(place_ref, wq, wq_scales, wkv, wkv_scales, *rest):
    outs, (q_levels, kv_levels) = rest[:4], rest[4:]
    q_levels[...] = wq_scales[...].astype(F32)
    kv_levels[...] = wkv_scales[...].astype(F32)
    for slot in range(4):
        out = outs[slot]

        def step(j, carry, slot=slot, out=out):
            chip, peer_c = source_block(place_ref, slot, j)
            q_both = q_levels[pl.ds(pl.multiple_of(chip * 4, 8), 8), :]
            kv_both = kv_levels[pl.ds(pl.multiple_of(chip * 4, 8), 8), :]
            for e in range(2):
                c = peer_c ^ e
                rows = pl.ds(pl.multiple_of((chip + c) * 128, 128), 128)
                level = jnp.where(c == 0, q_both[:4], q_both[4:])
                block = wq[rows, :].astype(F32).reshape(4, 32, 128) * level[:, None, :]
                to = pl.multiple_of((2 * j + e) * 128, 128)
                out[pl.ds(to, 128), :] = block.reshape(128, 128).astype(BF16)
                level = jnp.where(c == 0, kv_both[:4], kv_both[4:])
                block = wkv[rows, :].astype(F32).reshape(4, 32, KV) * level[:, None, :]
                to = pl.multiple_of(BLOCKS * 128 + (2 * j + e) * KV, KV)
                out[pl.ds(to, KV), :] = block.reshape(128, KV).T.astype(BF16)
            return carry

        lax.fori_loop(0, STEPS, step, 0)


def output_kernel(place_ref, wo, wo_scales, *outs):
    for slot in range(4):
        out = outs[slot]

        def step(j, carry, slot=slot, out=out):
            chip, peer_c = source_block(place_ref, slot, j)
            for e in range(2):
                columns = pl.ds(pl.multiple_of((chip + (peer_c ^ e)) * 128, 128), 128)
                level = wo_scales[:, columns].astype(F32)
                block = wo[:, columns].astype(F32).reshape(4, 32, 128) * level[:, None, :]
                to = pl.multiple_of((2 * j + e) * 128, 128)
                out[pl.ds(to, 128), :] = block.reshape(128, 128).astype(BF16)
            return carry

        lax.fori_loop(0, STEPS, step, 0)


def product_kernel(place_ref, *refs):
    pieces, grads = refs[: STEPS + 1], refs[STEPS + 1 : 2 * STEPS + 2]
    refs = refs[2 * STEPS + 2 :]
    projections, outputs, (kept, sent) = refs[:4], refs[4:8], refs[8:]
    first = place_ref[2] == 0
    base = LENGTH + 2 * RANK

    def pick(refs, start, rows):
        blocks = []
        for j in range(STEPS):
            for e in range(2):
                at = slice(e * refs[0].shape[0] // 2 + start, e * refs[0].shape[0] // 2 + start + rows)
                if j < STEPS - 1:
                    blocks.append(refs[j + 1][at])
                else:
                    blocks.append(jnp.where(first, refs[0][at], refs[STEPS][at]))
        return blocks

    inputs = jnp.concatenate(pick(pieces, 0, LENGTH), axis=1)
    downs = jnp.concatenate(pick(pieces, LENGTH, 2 * RANK), axis=1)
    squares = sum(
        b[0:2].astype(F32) + b[2:4].astype(F32) for b in pick(pieces, base, 16)
    )
    gradients = jnp.concatenate(pick(grads, 0, LENGTH), axis=1)
    low = contract(inputs, downs, 1, 1)
    kv_weights = jnp.concatenate(
        [
            jnp.concatenate(
                [p[BLOCKS * 128 + b * KV : BLOCKS * 128 + (b + 1) * KV, :] for b in range(BLOCKS)], axis=1
            )
            for p in projections
        ],
        axis=0,
    )
    kv = contract(kv_weights, inputs, 1, 1)
    for place_at, (out, cast) in enumerate(((kept, F32), (sent, BF16))):
        slots = (place_at, 2 + place_at)
        q_weights = jnp.concatenate([projections[s][: BLOCKS * 128, :] for s in slots], axis=1)
        q = contract(inputs, q_weights, 1, 0)
        o_weights = jnp.concatenate(
            [
                jnp.concatenate([outputs[s][b * 128 : (b + 1) * 128, :] for b in range(BLOCKS)], axis=1)
                for s in slots
            ],
            axis=0,
        )
        ctx = contract(gradients, o_weights, 1, 1)
        for i, s in enumerate(slots):
            at = i * PER_HEAD
            out[at : at + LENGTH] = q[:, i * 128 : (i + 1) * 128].astype(cast)
            out[at + LENGTH : at + 2 * LENGTH] = ctx[:, i * 128 : (i + 1) * 128].astype(cast)
            own = kv[s * KV : (s + 1) * KV]
            out[at + 2 * LENGTH : at + 2 * LENGTH + KV] = own[:, :128].astype(cast)
            out[at + 2 * LENGTH + KV : at + PER_HEAD] = own[:, 128:].astype(cast)
        at = 2 * PER_HEAD
        out[at : at + LENGTH] = low.astype(cast)
        high, rest = two_terms(squares)
        pad = jnp.zeros((12, 128), F32)
        out[at + LENGTH : at + SHARED] = jnp.concatenate(
            [high.astype(F32), rest.astype(F32), pad], axis=0
        ).astype(cast)


def middle_kernel(kept, got, keep, send):
    head, shared = kept[:PER_HEAD] + got[:PER_HEAD].astype(F32), 2 * PER_HEAD
    keep[:PER_HEAD] = head
    send[:PER_HEAD] = (kept[PER_HEAD:shared] + got[PER_HEAD:shared].astype(F32)).astype(BF16)
    low = kept[shared : shared + LENGTH] + got[shared : shared + LENGTH].astype(F32)
    keep[PER_HEAD : PER_HEAD + LENGTH] = low
    send[PER_HEAD : PER_HEAD + LENGTH] = low.astype(BF16)
    rows = kept[shared + LENGTH :] + got[shared + LENGTH :].astype(F32)
    squares = rows[0:2] + rows[2:4]
    high, rest = two_terms(squares)
    pad = jnp.zeros((12, 128), F32)
    rows = jnp.concatenate([high.astype(F32), rest.astype(F32), pad], axis=0)
    keep[PER_HEAD + LENGTH :] = rows
    send[PER_HEAD + LENGTH :] = rows.astype(BF16)


def turn(values, cosine, sine, axis):
    half = HEAD // 2
    if axis == 1:
        front, back = values[:, :half], values[:, half:]
    else:
        front, back = values[:half], values[half:]
    return jnp.concatenate([front * cosine - back * sine, back * cosine + front * sine], axis=axis)


def head_kernel(
    kept, got, hidden, gain, columns, own_columns, query_up, cosine, sine, queries, ctx, lows, normed, parcel
):
    total = kept[...] + got[...].astype(F32)
    q, grads = total[:LENGTH], total[LENGTH : 2 * LENGTH]
    kv = total[2 * LENGTH : PER_HEAD]
    low = total[PER_HEAD : PER_HEAD + LENGTH]
    squares = total[PER_HEAD + LENGTH : PER_HEAD + LENGTH + 2]
    squares = squares + total[PER_HEAD + LENGTH + 2 : PER_HEAD + LENGTH + 4]
    inverse = lax.rsqrt(squares * (1.0 / FEATURES) + EPS)
    column = jnp.concatenate([to_column(inverse[0:1]), to_column(inverse[1:2])], axis=0)
    normed[...] = (hidden[...].astype(F32) * column * gain[...].astype(F32)).astype(BF16)
    both = (low * column).astype(BF16)
    lows[...] = both
    ctx[...] = grads.astype(BF16)
    linear = q * column + ADAPTER_SCALE * contract(both[:, :RANK], query_up[...], 1, 0)
    queries[...] = turn(linear, cosine[...], sine[...], 1).astype(BF16)
    adapter = ADAPTER_SCALE * contract(columns[:, :RANK], both[:, RANK:], 1, 1)
    first = (kv[:KV] * inverse[0:1] + adapter[:, :128]).astype(BF16)
    second = (kv[KV:] * inverse[1:2] + adapter[:, 128:]).astype(BF16)
    mine = jnp.concatenate([first, second, own_columns[...]], axis=0)
    for i in range(GROUP):
        parcel[i] = mine


def attention_kernel(
    group, queries, ctx, lows, query_up, cosine, sine, cosine_t, sine_t, snapshot_row, snapshot_column, out, up
):
    def side(start):
        return jnp.concatenate(
            [
                jnp.concatenate([group[p, :KV, :], group[p, KV : 2 * KV, :]], axis=1)
                for p in range(start, start + 4)
            ],
            axis=0,
        )

    keys = turn(side(0).astype(F32), cosine_t[...], sine_t[...], 0).astype(BF16)
    values = side(4)
    value_up = jnp.concatenate([group[p, 2 * KV :, :] for p in range(GROUP)], axis=0)[:, :RANK]
    scale = HEAD ** (-0.5)
    scores = contract(queries[...], keys, 1, 0) * scale
    row = lax.broadcasted_iota(jnp.int32, (LENGTH, LENGTH), 0)
    column = lax.broadcasted_iota(jnp.int32, (LENGTH, LENGTH), 1)
    allowed = jnp.logical_and(column <= row, snapshot_column[...] == snapshot_row[...])
    scores = jnp.where(allowed, scores, MASKED)
    weights = jnp.exp(scores - jnp.max(scores, axis=1, keepdims=True))
    prob = weights / jnp.sum(weights, axis=1, keepdims=True)
    grads = ctx[...]
    grad_prob = contract(grads, values, 1, 0)
    grad_value = contract(prob.astype(BF16), grads, 0, 0).astype(BF16)
    inner = jnp.sum(prob * grad_prob, axis=1, keepdims=True)
    grad_score = (prob * (grad_prob - inner)).astype(BF16)
    grad_query = contract(grad_score, keys, 1, 1) * scale
    grad_linear = turn(grad_query, cosine[...], -sine[...], 1).astype(BF16)
    low_q, low_v = lows[:, :RANK], lows[:, RANK:]
    up[...] = ADAPTER_SCALE * contract(low_q, grad_linear, 0, 0)
    slices = ADAPTER_SCALE * contract(grad_value, low_v, 0, 0)
    slices = jnp.concatenate([slices, jnp.zeros((HEAD, 128 - RANK), F32)], axis=1).astype(BF16)
    grad_low = jnp.concatenate(
        [
            ADAPTER_SCALE * contract(grad_linear, query_up[...], 1, 1),
            ADAPTER_SCALE * contract(grad_value, value_up, 1, 0),
        ],
        axis=1,
    ).astype(BF16)
    rows = LENGTH // GROUP
    for i in range(GROUP):
        out[i, :rows, :] = grad_low[i * rows : (i + 1) * rows]
        out[i, rows:, :] = slices[16 * i : 16 * i + 16]


def near_kernel(parts, low, value):
    total = jnp.sum(parts[...].astype(F32), axis=0)
    rows = LENGTH // GROUP
    value[...] = total[rows:]
    for i in range(8):
        low[i] = total[:rows].astype(BF16)


def far_kernel(parts, low):
    total = jnp.sum(parts[...].astype(F32), axis=0).astype(BF16)
    for i in range(GROUP):
        low[i] = total


def rows_kernel(normed, low, up, value, out):
    whole = jnp.concatenate([low[i] for i in range(GROUP)], axis=0)
    rows = contract(normed[...], whole, 0, 0).astype(BF16)
    last = jnp.concatenate([up[...], value[...]], axis=0).astype(BF16)
    for i in range(8):
        out[i, :HEAD, :] = rows
        out[i, HEAD:, :] = last


def total_kernel(parts, grad_a_query, query_up, grad_a_value, value):
    total = jnp.sum(parts[...].astype(F32), axis=0)
    grad_a_query[...] = total[:HEAD, :RANK]
    grad_a_value[...] = total[:HEAD, RANK:]
    query_up[...] = total[HEAD : HEAD + RANK]
    value[...] = total[HEAD + RANK :, :RANK].T


def local(
    hidden_in,
    out_grad,
    snapshot_ids,
    norm_gain,
    wq_codes,
    wq_scales,
    wkv_codes,
    wkv_scales,
    wo_codes,
    wo_scales,
    a_query,
    query_up_weight,
    a_value,
    value_up_weight,
):
    head_index = lax.axis_index("fsdp")
    core = head_index % NC
    spot = jnp.stack([head_index // (NZ * NC), head_index // NC % NZ, core]).astype(jnp.int32)
    gain = norm_gain[None, :]

    packet = call(pack_kernel, shape(PACKET + 16, 128), hidden_in, gain, a_query, a_value, value_up_weight)
    other = swap(packet, 1)
    other_grad = swap(out_grad, 1)
    pieces = [jnp.concatenate([packet[:PACKET], other[:PACKET]], axis=0)]
    grads = [jnp.concatenate([out_grad, other_grad], axis=0)]
    for step in range(STEPS):
        pairs = RING if step < STEPS - 1 else LAST
        pieces.append(lax.ppermute(pieces[-1], "fsdp", pairs))
        grads.append(lax.ppermute(grads[-1], "fsdp", pairs))

    own_columns, other_columns = packet[PACKET:], other[PACKET:]
    chip_columns = jnp.where(
        core == 0,
        jnp.concatenate([own_columns, other_columns], axis=0),
        jnp.concatenate([other_columns, own_columns], axis=0),
    )
    columns = lax.ppermute(after(chip_columns, pieces[5]), "fsdp", TO_MEMBER)

    rows = BLOCKS * (128 + KV)
    projections = call(
        projection_kernel,
        [shape(rows, 128)] * 4,
        spot,
        after(wq_codes, packet),
        wq_scales,
        wkv_codes,
        wkv_scales,
        scratch=[pltpu.VMEM((256, 128), F32), pltpu.VMEM((256, KV), F32)],
    )
    outputs = call(
        output_kernel, [shape(BLOCKS * 128, 128)] * 4, spot, after(wo_codes, pieces[1]), wo_scales
    )
    masks = (1, NZ * NC, NZ * NC + 1)
    projections = [projections[0]] + [
        swap(after(projections[s], pieces[w]), masks[s - 1]) for s, w in ((1, 2), (2, 0), (3, 1))
    ]
    outputs = [outputs[0]] + [
        swap(after(outputs[s], pieces[w]), masks[s - 1]) for s, w in ((1, 5), (2, 3), (3, 4))
    ]

    rows = 2 * PER_HEAD + SHARED
    kept, sent = call(
        product_kernel,
        [shape(rows, 128, dtype=F32), shape(rows, 128)],
        spot,
        *pieces,
        *grads,
        *projections,
        *outputs,
        megabytes=48,
    )
    rows = PER_HEAD + SHARED
    kept, sent = call(middle_kernel, [shape(rows, 128, dtype=F32), shape(rows, 128)], kept, swap(sent, 1))
    got = swap(sent, NZ * NC)

    cosine, sine = rope_tables()
    square = shape(LENGTH, 128)
    queries, ctx, lows, normed, parcel = call(
        head_kernel,
        [square, square, square, square, shape(GROUP, 2 * KV + 16, 128)],
        kept,
        got,
        hidden_in,
        gain,
        columns,
        own_columns,
        query_up_weight,
        jnp.asarray(cosine),
        jnp.asarray(sine),
    )
    group = exchange(parcel, "fsdp", NEAR_GROUPS)
    slices, up = call(
        attention_kernel,
        [shape(GROUP, LENGTH // GROUP + 16, 128), shape(RANK, HEAD, dtype=F32)],
        group,
        queries,
        ctx,
        lows,
        query_up_weight,
        jnp.asarray(cosine),
        jnp.asarray(sine),
        jnp.asarray(cosine.T.copy()),
        jnp.asarray(sine.T.copy()),
        snapshot_ids,
        snapshot_ids.reshape(LENGTH, 1),
    )

    low, value = call(
        near_kernel,
        [shape(8, LENGTH // GROUP, 128), shape(16, 128, dtype=F32)],
        exchange(slices, "fsdp", NEAR_GROUPS),
    )
    low = call(far_kernel, shape(GROUP, LENGTH // GROUP, 128), exchange(low, "fsdp", FAR_GROUPS))
    mine = call(
        rows_kernel,
        shape(8, HEAD + RANK + 16, 128),
        normed,
        exchange(low, "fsdp", NEAR_GROUPS),
        up,
        value,
    )
    return tuple(
        call(
            total_kernel,
            [
                shape(HEAD, RANK, dtype=F32),
                shape(RANK, HEAD, dtype=F32),
                shape(HEAD, RANK, dtype=F32),
                shape(RANK, 16, dtype=F32),
            ],
            exchange(mine, "dp"),
        )
    )


def solution(mesh):
    in_specs = (
        P("dp", "fsdp"),
        P("dp", "fsdp"),
        P("dp", None),
        P("fsdp"),
        P(None, "fsdp"),
        P(None, "fsdp"),
        P(None, "fsdp"),
        P(None, "fsdp"),
        P("fsdp", None),
        P("fsdp", None),
        P(None, "fsdp"),
        P(None, "fsdp"),
        P(None, "fsdp"),
        P(None, "fsdp"),
    )
    out_specs = (P("fsdp", None), P(None, "fsdp"), P("fsdp", None), P(None, "fsdp"))
    return jax.shard_map(local, mesh=mesh, in_specs=in_specs, out_specs=out_specs, check_vma=False)
```

```python
import math

import jax
import jax.numpy as jnp
import numpy as np
from jax import lax
from jax.experimental import pallas as pl
from jax.experimental.pallas import tpu as pltpu
from jax.sharding import PartitionSpec as P

GROUP = 8
EPS = 1e-05
ADAPTER_SCALE = 0.5
ROPE_BASE = 500000.0
MASKED = -1e30

NX, NZ, NC = 2, 16, 2
LENGTH, HEAD, RANK, KV = 256, 128, 64, 32
FEATURES = NX * NZ * NC * HEAD
BLOCKS = NZ
DOWNS_AT = LENGTH
SQUARES_AT = DOWNS_AT + 2 * RANK
COLUMNS_AT = SQUARES_AT + 16
GRADS_AT = COLUMNS_AT + 16
PACKET = GRADS_AT + LENGTH
PER_HEAD = 2 * LENGTH
SHARED = LENGTH + 16

F32, BF16 = jnp.float32, jnp.bfloat16
VMEM = pl.BlockSpec(memory_space=pltpu.VMEM)
SMEM = pl.BlockSpec(memory_space=pltpu.SMEM)


def place(a, z, c):
    return a * (NZ * NC) + z * NC + c


Z_GROUPS = [[place(a, z, c) for z in range(NZ)] for a in range(NX) for c in range(NC)]
BOX_GROUPS = [
    [place(a, 4 * b + i, c) for a in range(NX) for i in range(4) for c in range(NC)] for b in range(4)
]
NEAR_GROUPS = [[GROUP * g + i for i in range(GROUP)] for g in range(8)]
FAR_GROUPS = [
    [place(a, z + 4 * k, c) for a in range(NX) for k in range(4)] for z in range(4) for c in range(NC)
]


def swap(value, mask):
    return lax.ppermute(value, "fsdp", [(i, i ^ mask) for i in range(NX * NZ * NC)])


def swap_weights(value, mask):
    if mask < NZ * NC:
        return swap(value, mask)
    size = NX * NZ * NC
    rows = lax.axis_size("dp")
    pairs = [(d * size + i, (d ^ 1) * size + (i ^ mask)) for d in range(rows) for i in range(size)]
    return lax.ppermute(value, ("dp", "fsdp"), pairs)


def exchange(value, axis, groups=None):
    return lax.all_to_all(value, axis, 0, 0, axis_index_groups=groups)


def after(value, *others):
    return lax.optimization_barrier((value, *others))[0]


def rope_tables():
    positions = np.arange(LENGTH, dtype=np.float32)[:, None]
    steps = np.arange(HEAD // 2, dtype=np.float32)
    frequency = np.exp(steps * np.float32(-2.0 * math.log(ROPE_BASE) / HEAD)).astype(np.float32)
    angles = positions * frequency[None, :]
    return np.cos(angles).astype(np.float32), np.sin(angles).astype(np.float32)


def contract(left_arr, right_arr, left_dim, right_dim):
    return lax.dot_general(
        left_arr,
        right_arr,
        (((left_dim,), (right_dim,)), ((), ())),
        preferred_element_type=F32,
    )


def two_terms(value):
    high = value.astype(BF16)
    return high, (value - high.astype(F32)).astype(BF16)


def call(body, outs, *operands, scratch=(), megabytes=32, held=False):
    specs = [SMEM if o.dtype == jnp.int32 and o.ndim == 1 else VMEM for o in operands]
    if held:
        specs = [spec if spec is SMEM else pl.BlockSpec(memory_space=pl.ANY) for spec in specs]
    many = isinstance(outs, (list, tuple))
    return pl.pallas_call(
        body,
        out_shape=outs,
        in_specs=specs,
        out_specs=[VMEM] * len(outs) if many else VMEM,
        scratch_shapes=list(scratch),
        compiler_params=pltpu.CompilerParams(vmem_limit_bytes=megabytes << 20),
    )(*operands)


def shape(*dims, dtype=BF16):
    return jax.ShapeDtypeStruct(dims, dtype)


def diagonal(size):
    return lax.broadcasted_iota(jnp.int32, (size, size), 0) == lax.broadcasted_iota(
        jnp.int32, (size, size), 1
    )


def to_row(column):
    return jnp.sum(jnp.where(diagonal(128), column, 0.0), axis=0, keepdims=True)


def to_column(row):
    return jnp.sum(jnp.where(diagonal(128), row, 0.0), axis=1, keepdims=True)


def fetch(sources, targets, sems):
    copies = [pltpu.make_async_copy(a, b, sems.at[i]) for i, (a, b) in enumerate(zip(sources, targets))]
    for copy in copies:
        copy.start()
    for copy in copies:
        copy.wait()


def pack_kernel(
    hidden_at, gain_at, a_query_at, a_value_at, value_up_at, grad_at, packet, hidden, gain, value_up, sems
):
    fetch(
        (hidden_at, gain_at, value_up_at, a_query_at, a_value_at, grad_at),
        (
            hidden,
            gain,
            value_up,
            packet.at[pl.ds(DOWNS_AT, RANK)],
            packet.at[pl.ds(DOWNS_AT + RANK, RANK)],
            packet.at[pl.ds(GRADS_AT, LENGTH)],
        ),
        sems,
    )
    values = hidden[...].astype(F32)
    packet[:LENGTH] = (values * gain[...].astype(F32)).astype(BF16)
    squares = jnp.sum(values * values, axis=1, keepdims=True)
    rows = jnp.concatenate([to_row(squares[:128]), to_row(squares[128:])], axis=0)
    high, low = two_terms(rows)
    packet[SQUARES_AT:COLUMNS_AT] = jnp.concatenate([high, low, jnp.zeros((12, 128), BF16)], axis=0)
    packet[COLUMNS_AT:GRADS_AT] = jnp.concatenate(
        [value_up[...], jnp.zeros((16, 128 - RANK), BF16)], axis=1
    )


def peer_block(place_ref, slot, j):
    peer_x = place_ref[0] ^ (slot >> 1)
    peer_c = place_ref[2] ^ (slot & 1)
    return peer_x * (NZ * NC) + j * NC + peer_c, peer_c


def projection_kernel(place_ref, *rest):
    sources, outs, held = rest[:4], rest[4:8], rest[8:12]
    q_levels, kv_levels, sems = rest[12:]
    fetch(sources, held, sems)
    wq, wq_scales, wkv, wkv_scales = held
    q_levels[...] = wq_scales[...].astype(F32)
    widen = lax.broadcasted_iota(jnp.int32, (32, 1024), 1) // 32 == lax.broadcasted_iota(
        jnp.int32, (32, 1024), 0
    )
    widen = jnp.where(widen, 1.0, 0.0).astype(BF16)
    for i in range(8):
        level = contract(wkv_scales[:, 32 * i : 32 * i + 32], widen, 1, 0)
        kv_levels[:, 1024 * i : 1024 * i + 1024] = level
    for slot in range(4):
        out = outs[slot]

        def step(j, carry, slot=slot, out=out):
            block, peer_c = peer_block(place_ref, slot, j)
            rows = pl.ds(pl.multiple_of(block * 128, 128), 128)
            both = q_levels[pl.ds(pl.multiple_of((block - peer_c) * 4, 8), 8), :]
            level = jnp.where(peer_c == 0, both[:4], both[4:])
            codes = wq[rows, :].astype(F32).reshape(4, 32, 128) * level[:, None, :]
            to = pl.multiple_of(j * 128, 128)
            out[pl.ds(to, 128), :] = codes.reshape(128, 128).astype(BF16)
            codes = wkv[:, rows].astype(F32) * kv_levels[:, rows]
            to = pl.multiple_of(BLOCKS * 128 + j * KV, KV)
            out[pl.ds(to, KV), :] = codes.astype(BF16)
            return carry

        lax.fori_loop(0, BLOCKS, step, 0, unroll=2)


def output_kernel(place_ref, *rest):
    sources, outs, (wo, wo_scales, sems) = rest[:2], rest[2:6], rest[6:]
    fetch(sources, (wo, wo_scales), sems)
    for slot in range(4):
        out = outs[slot]

        def step(j, carry, slot=slot, out=out):
            block, _ = peer_block(place_ref, slot, j)
            columns = pl.ds(pl.multiple_of(block * 128, 128), 128)
            level = wo_scales[:, columns].astype(F32)
            codes = wo[:, columns].astype(F32).reshape(4, 32, 128) * level[:, None, :]
            to = pl.multiple_of(j * 128, 128)
            out[pl.ds(to, 128), :] = codes.reshape(128, 128).astype(BF16)
            return carry

        lax.fori_loop(0, BLOCKS, step, 0, unroll=2)


def product_kernel(place_ref, gathered, *refs):
    weights, outputs, (kept, sent, box) = refs[:4], refs[4:8], refs[8:]
    inputs = gathered[:LENGTH]
    low = contract(inputs, gathered[DOWNS_AT:SQUARES_AT], 1, 1)
    squares = sum(
        gathered[SQUARES_AT : SQUARES_AT + 16, b * 128 : (b + 1) * 128].astype(F32) for b in range(BLOCKS)
    )
    squares = squares[0:2] + squares[2:4]
    kv_weights = jnp.concatenate(
        [
            jnp.concatenate(
                [w[BLOCKS * 128 + b * KV : BLOCKS * 128 + (b + 1) * KV, :] for b in range(BLOCKS)], axis=1
            )
            for w in weights
        ],
        axis=0,
    )
    kv = contract(kv_weights, inputs, 1, 1).astype(BF16)
    at_zero, first = place_ref[0] == 0, place_ref[2] == 0
    for a in range(NX):
        mine = at_zero if a == 0 else jnp.logical_not(at_zero)
        near = jnp.where(mine, kv[: 2 * KV], kv[2 * KV :])
        low_core = jnp.where(first, near[:KV], near[KV:])
        high_core = jnp.where(first, near[KV:], near[:KV])
        whole = jnp.concatenate(
            [low_core[:, :128], low_core[:, 128:], high_core[:, :128], high_core[:, 128:]], axis=0
        )
        for i in range(GROUP):
            box[GROUP * a + i] = whole
    block_start = pl.multiple_of(place_ref[1] // 4 * 512, 512)
    columns = gathered[COLUMNS_AT:GRADS_AT, pl.ds(block_start, 512)]
    columns = jnp.concatenate([columns[:, 128 * i : 128 * i + 128] for i in range(4)], axis=0)
    gradients = gathered[GRADS_AT:]
    for place_at, (out, cast) in enumerate(((kept, F32), (sent, BF16))):
        slots = (place_at, 2 + place_at)
        q_weights = jnp.concatenate([weights[s][: BLOCKS * 128, :] for s in slots], axis=1)
        q = contract(inputs, q_weights, 1, 0)
        o_weights = jnp.concatenate(
            [
                jnp.concatenate([outputs[s][b * 128 : (b + 1) * 128, :] for b in range(BLOCKS)], axis=1)
                for s in slots
            ],
            axis=0,
        )
        ctx = contract(gradients, o_weights, 1, 1)
        for i in range(2):
            at = i * PER_HEAD
            out[at : at + LENGTH] = q[:, i * 128 : (i + 1) * 128].astype(cast)
            out[at + LENGTH : at + PER_HEAD] = ctx[:, i * 128 : (i + 1) * 128].astype(cast)
        at = 2 * PER_HEAD
        out[at : at + LENGTH] = low.astype(cast)
        high, rest = two_terms(squares)
        pad = jnp.zeros((12, 128), F32)
        out[at + LENGTH : at + SHARED] = jnp.concatenate(
            [high.astype(F32), rest.astype(F32), pad], axis=0
        ).astype(cast)
        out[at + SHARED :] = columns.astype(cast)


def middle_kernel(place_ref, kept, got, keep, send, value_up):
    shared = 2 * PER_HEAD
    keep[:PER_HEAD] = kept[:PER_HEAD] + got[:PER_HEAD].astype(F32)
    send[:PER_HEAD] = (kept[PER_HEAD:shared] + got[PER_HEAD:shared].astype(F32)).astype(BF16)
    low = kept[shared : shared + LENGTH] + got[shared : shared + LENGTH].astype(F32)
    keep[PER_HEAD : PER_HEAD + LENGTH] = low
    send[PER_HEAD : PER_HEAD + LENGTH] = low.astype(BF16)
    rows = kept[shared + LENGTH : shared + SHARED] + got[shared + LENGTH : shared + SHARED].astype(F32)
    squares = rows[0:2] + rows[2:4]
    high, rest = two_terms(squares)
    pad = jnp.zeros((12, 128), F32)
    rows = jnp.concatenate([high.astype(F32), rest.astype(F32), pad], axis=0)
    keep[PER_HEAD + LENGTH :] = rows
    send[PER_HEAD + LENGTH :] = rows.astype(BF16)
    mine, other = kept[shared + SHARED :].astype(BF16), got[shared + SHARED :]
    first = place_ref[2] == 0
    for i in range(4):
        own, its = mine[16 * i : 16 * i + 16], other[16 * i : 16 * i + 16]
        value_up[32 * i : 32 * i + 16] = jnp.where(first, own, its)
        value_up[32 * i + 16 : 32 * i + 32] = jnp.where(first, its, own)


def turn(values, cosine, sine, axis):
    half = HEAD // 2
    if axis == 1:
        front, back = values[:, :half], values[:, half:]
    else:
        front, back = values[:half], values[half:]
    return jnp.concatenate([front * cosine - back * sine, back * cosine + front * sine], axis=axis)


def attention_kernel(
    kept,
    got,
    box,
    value_up_ref,
    hidden,
    gain,
    query_up,
    cosine,
    sine,
    cosine_t,
    sine_t,
    snapshot,
    out,
    up,
    normed,
):
    total = kept[...] + got[...].astype(F32)
    low = total[PER_HEAD : PER_HEAD + LENGTH]
    squares = total[PER_HEAD + LENGTH : PER_HEAD + LENGTH + 2]
    squares = squares + total[PER_HEAD + LENGTH + 2 : PER_HEAD + LENGTH + 4]
    inverse = lax.rsqrt(squares * (1.0 / FEATURES) + EPS)
    column = jnp.concatenate([to_column(inverse[0:1]), to_column(inverse[1:2])], axis=0)
    normed[...] = (hidden[...].astype(F32) * column * gain[...].astype(F32)).astype(BF16)
    lows = (low * column).astype(BF16)
    linear = total[:LENGTH] * column + ADAPTER_SCALE * contract(lows[:, :RANK], query_up[...], 1, 0)
    queries = turn(linear, cosine[...], sine[...], 1).astype(BF16)
    grads = total[LENGTH:PER_HEAD].astype(BF16)
    row_inverse = jnp.concatenate([inverse[0:1], inverse[1:2]], axis=1)
    value_up = value_up_ref[:, :RANK]

    def side(start):
        rows = []
        for i in (start, start + 1):
            part = sum(box[GROUP * a + 2 * i + c].astype(F32) for a in range(NX) for c in range(NC))
            for c in range(NC):
                at = 2 * KV * c
                rows.append(jnp.concatenate([part[at : at + KV], part[at + KV : at + 2 * KV]], axis=1))
        return jnp.concatenate(rows, axis=0) * row_inverse

    keys = side(0).astype(BF16).astype(F32)
    keys = turn(keys, cosine_t[...], sine_t[...], 0).astype(BF16)
    values = (side(2) + ADAPTER_SCALE * contract(value_up, lows[:, RANK:], 1, 1)).astype(BF16)
    scale = HEAD ** (-0.5)
    scores = contract(queries, keys, 1, 0) * scale
    row = lax.broadcasted_iota(jnp.int32, (LENGTH, LENGTH), 0)
    column = lax.broadcasted_iota(jnp.int32, (LENGTH, LENGTH), 1)
    segment = snapshot[...].astype(F32)
    own = jnp.concatenate([to_column(segment[:, :128]), to_column(segment[:, 128:])], axis=0)
    allowed = jnp.logical_and(column <= row, own == segment)
    scores = jnp.where(allowed, scores, MASKED)
    weights = jnp.exp(scores - jnp.max(scores, axis=1, keepdims=True))
    prob = weights / jnp.sum(weights, axis=1, keepdims=True)
    grad_prob = contract(grads, values, 1, 0)
    grad_value = contract(prob.astype(BF16), grads, 0, 0).astype(BF16)
    inner = jnp.sum(prob * grad_prob, axis=1, keepdims=True)
    grad_score = (prob * (grad_prob - inner)).astype(BF16)
    grad_query = contract(grad_score, keys, 1, 1) * scale
    grad_linear = turn(grad_query, cosine[...], -sine[...], 1).astype(BF16)
    low_q, low_v = lows[:, :RANK], lows[:, RANK:]
    up[...] = ADAPTER_SCALE * contract(low_q, grad_linear, 0, 0)
    slices = ADAPTER_SCALE * contract(grad_value, low_v, 0, 0)
    slices = jnp.concatenate([slices, jnp.zeros((HEAD, 128 - RANK), F32)], axis=1).astype(BF16)
    grad_low = jnp.concatenate(
        [
            ADAPTER_SCALE * contract(grad_linear, query_up[...], 1, 1),
            ADAPTER_SCALE * contract(grad_value, value_up, 1, 0),
        ],
        axis=1,
    ).astype(BF16)
    rows = LENGTH // GROUP
    for i in range(GROUP):
        out[i, :rows, :] = grad_low[i * rows : (i + 1) * rows]
        out[i, rows:, :] = slices[16 * i : 16 * i + 16]


def near_kernel(parts, low, value):
    total = jnp.sum(parts[...].astype(F32), axis=0)
    rows = LENGTH // GROUP
    value[...] = total[rows:]
    for i in range(8):
        low[i] = total[:rows].astype(BF16)


def far_kernel(parts, low):
    total = jnp.sum(parts[...].astype(F32), axis=0).astype(BF16)
    for i in range(GROUP):
        low[i] = total


def rows_kernel(normed, low, up, value, out):
    whole = jnp.concatenate([low[i] for i in range(GROUP)], axis=0)
    rows = contract(normed[...], whole, 0, 0).astype(BF16)
    last = jnp.concatenate([up[...], value[...]], axis=0).astype(BF16)
    for i in range(8):
        out[i, :HEAD, :] = rows
        out[i, HEAD:, :] = last


def total_kernel(parts, grad_a_query, query_up, grad_a_value, value):
    total = jnp.sum(parts[...].astype(F32), axis=0)
    rows = total[:HEAD].T
    grad_a_query[...] = rows[:RANK]
    grad_a_value[...] = rows[RANK:]
    query_up[...] = total[HEAD : HEAD + RANK]
    value[...] = total[HEAD + RANK :, :RANK]


def local(
    hidden_in,
    out_grad,
    snapshot_ids,
    norm_gain,
    wq_codes,
    wq_scales,
    wkv_codes,
    wkv_scales,
    wo_codes,
    wo_scales,
    a_query,
    query_up_weight,
    a_value,
    value_up_weight,
):
    head_index = lax.axis_index("fsdp")
    spot = jnp.stack([head_index // (NZ * NC), head_index // NC % NZ, head_index % NC]).astype(jnp.int32)
    gain = norm_gain[None, :]
    masks = (1, NZ * NC, NZ * NC + 1)

    packet = call(
        pack_kernel,
        shape(PACKET, 128),
        hidden_in,
        gain,
        a_query,
        a_value,
        value_up_weight.T,
        out_grad,
        scratch=[
            pltpu.VMEM((LENGTH, 128), BF16),
            pltpu.VMEM((1, 128), BF16),
            pltpu.VMEM((16, RANK), BF16),
            pltpu.SemaphoreType.DMA((6,)),
        ],
        megabytes=56,
        held=True,
    )
    gathered = lax.all_gather(packet, "fsdp", axis=1, tiled=True, axis_index_groups=Z_GROUPS)

    spot = after(spot, packet)
    projections = call(
        projection_kernel,
        [shape(BLOCKS * (128 + KV), 128)] * 4,
        spot,
        wq_codes,
        wq_scales,
        wkv_codes.T,
        wkv_scales.T,
        scratch=[
            pltpu.VMEM((FEATURES, 128), BF16),
            pltpu.VMEM((256, 128), BF16),
            pltpu.VMEM((KV, FEATURES), BF16),
            pltpu.VMEM((KV, 256), BF16),
            pltpu.VMEM((256, 128), F32),
            pltpu.VMEM((KV, FEATURES), F32),
            pltpu.SemaphoreType.DMA((4,)),
        ],
        megabytes=56,
        held=True,
    )
    outputs = call(
        output_kernel,
        [shape(BLOCKS * 128, 128)] * 4,
        after(spot, *projections),
        wo_codes,
        wo_scales,
        scratch=[
            pltpu.VMEM((128, FEATURES), BF16),
            pltpu.VMEM((4, FEATURES), BF16),
            pltpu.SemaphoreType.DMA((2,)),
        ],
        megabytes=56,
        held=True,
    )
    projections = [projections[0]] + [swap_weights(p, mask) for p, mask in zip(projections[1:], masks)]
    outputs = [outputs[0]] + [swap_weights(p, mask) for p, mask in zip(outputs[1:], masks)]

    rows = 2 * PER_HEAD + SHARED + 64
    kept, sent, box = call(
        product_kernel,
        [shape(rows, 128, dtype=F32), shape(rows, 128), shape(2 * GROUP, 128, 128)],
        spot,
        gathered,
        *projections,
        *outputs,
        megabytes=56,
    )
    box = exchange(box, "fsdp", BOX_GROUPS)
    rows = PER_HEAD + SHARED
    kept, sent, value_up = call(
        middle_kernel,
        [shape(rows, 128, dtype=F32), shape(rows, 128), shape(128, 128)],
        spot,
        kept,
        swap(sent, 1),
    )
    got = swap(sent, NZ * NC)

    cosine, sine = rope_tables()
    slices, up, normed = call(
        attention_kernel,
        [shape(GROUP, LENGTH // GROUP + 16, 128), shape(RANK, HEAD, dtype=F32), shape(LENGTH, 128)],
        kept,
        got,
        box,
        value_up,
        hidden_in,
        gain,
        query_up_weight,
        jnp.asarray(cosine),
        jnp.asarray(sine),
        jnp.asarray(cosine.T.copy()),
        jnp.asarray(sine.T.copy()),
        snapshot_ids,
    )

    low, value = call(
        near_kernel,
        [shape(8, LENGTH // GROUP, 128), shape(16, 128, dtype=F32)],
        exchange(slices, "fsdp", NEAR_GROUPS),
    )
    low = call(far_kernel, shape(GROUP, LENGTH // GROUP, 128), exchange(low, "fsdp", FAR_GROUPS))
    mine = call(
        rows_kernel,
        shape(8, HEAD + RANK + 16, 128),
        normed,
        exchange(low, "fsdp", NEAR_GROUPS),
        up,
        value,
    )
    grad_a_query, query_up, grad_a_value, value = call(
        total_kernel,
        [
            shape(RANK, HEAD, dtype=F32),
            shape(RANK, HEAD, dtype=F32),
            shape(RANK, HEAD, dtype=F32),
            shape(16, RANK, dtype=F32),
        ],
        exchange(mine, "dp"),
    )
    return grad_a_query.T, query_up, grad_a_value.T, value.T


def solution(mesh):
    in_specs = (
        P("dp", "fsdp"),
        P("dp", "fsdp"),
        P("dp", None),
        P("fsdp"),
        P(None, "fsdp"),
        P(None, "fsdp"),
        P(None, "fsdp"),
        P(None, "fsdp"),
        P("fsdp", None),
        P("fsdp", None),
        P(None, "fsdp"),
        P(None, "fsdp"),
        P(None, "fsdp"),
        P(None, "fsdp"),
    )
    out_specs = (P("fsdp", None), P(None, "fsdp"), P("fsdp", None), P(None, "fsdp"))
    return jax.shard_map(local, mesh=mesh, in_specs=in_specs, out_specs=out_specs, check_vma=False)
```

```python
import math

import jax
import jax.numpy as jnp
import numpy as np
from jax import lax
from jax.experimental import pallas as pl
from jax.experimental.pallas import tpu as pltpu
from jax.sharding import PartitionSpec as P

GROUP = 8
EPS = 1e-05
ADAPTER_SCALE = 0.5
ROPE_BASE = 500000.0
MASKED = -1e30

NX, NZ, NC = 2, 16, 2
LENGTH, HEAD, RANK, KV = 256, 128, 64, 32
FEATURES = NX * NZ * NC * HEAD
HALF = FEATURES // NX
BLOCKS = NZ * NC
DOWNS_AT = LENGTH
SQUARES_AT = DOWNS_AT + 2 * RANK
COLUMNS_AT = SQUARES_AT + 16
GRADS_AT = COLUMNS_AT + 16
PACKET = GRADS_AT + LENGTH
PER_HEAD = 2 * LENGTH
SHARED = LENGTH + 16

F32, BF16 = jnp.float32, jnp.bfloat16
VMEM = pl.BlockSpec(memory_space=pltpu.VMEM)
SMEM = pl.BlockSpec(memory_space=pltpu.SMEM)


def place(a, z, c):
    return a * (NZ * NC) + z * NC + c


HALF_GROUPS = [[place(a, z, c) for z in range(NZ) for c in range(NC)] for a in range(NX)]
BOX_GROUPS = [
    [place(a, 4 * b + i, c) for a in range(NX) for i in range(4) for c in range(NC)] for b in range(4)
]
NEAR_GROUPS = [[GROUP * g + i for i in range(GROUP)] for g in range(8)]
FAR_GROUPS = [
    [place(a, z + 4 * k, c) for a in range(NX) for k in range(4)] for z in range(4) for c in range(NC)
]


def swap(value, mask):
    return lax.ppermute(value, "fsdp", [(i, i ^ mask) for i in range(NX * NZ * NC)])


def swap_weights(value, mask):
    if mask < NZ * NC:
        return swap(value, mask)
    size = NX * NZ * NC
    rows = lax.axis_size("dp")
    pairs = [(d * size + i, (d ^ 1) * size + (i ^ mask)) for d in range(rows) for i in range(size)]
    return lax.ppermute(value, ("dp", "fsdp"), pairs)


def exchange(value, axis, groups=None):
    return lax.all_to_all(value, axis, 0, 0, axis_index_groups=groups)


def after(value, *others):
    return lax.optimization_barrier((value, *others))[0]


def rope_tables():
    positions = np.arange(LENGTH, dtype=np.float32)[:, None]
    steps = np.arange(HEAD // 2, dtype=np.float32)
    frequency = np.exp(steps * np.float32(-2.0 * math.log(ROPE_BASE) / HEAD)).astype(np.float32)
    angles = positions * frequency[None, :]
    return np.cos(angles).astype(np.float32), np.sin(angles).astype(np.float32)


def contract(left_arr, right_arr, left_dim, right_dim):
    return lax.dot_general(
        left_arr,
        right_arr,
        (((left_dim,), (right_dim,)), ((), ())),
        preferred_element_type=F32,
    )


def two_terms(value):
    high = value.astype(BF16)
    return high, (value - high.astype(F32)).astype(BF16)


def call(body, outs, *operands, scratch=(), megabytes=32, held=False):
    specs = [SMEM if o.dtype == jnp.int32 and o.ndim == 1 else VMEM for o in operands]
    if held:
        specs = [spec if spec is SMEM else pl.BlockSpec(memory_space=pl.ANY) for spec in specs]
    many = isinstance(outs, (list, tuple))
    return pl.pallas_call(
        body,
        out_shape=outs,
        in_specs=specs,
        out_specs=[VMEM] * len(outs) if many else VMEM,
        scratch_shapes=list(scratch),
        compiler_params=pltpu.CompilerParams(vmem_limit_bytes=megabytes << 20),
    )(*operands)


def shape(*dims, dtype=BF16):
    return jax.ShapeDtypeStruct(dims, dtype)


def diagonal(size):
    return lax.broadcasted_iota(jnp.int32, (size, size), 0) == lax.broadcasted_iota(
        jnp.int32, (size, size), 1
    )


def to_row(column):
    return jnp.sum(jnp.where(diagonal(128), column, 0.0), axis=0, keepdims=True)


def to_column(row):
    return jnp.sum(jnp.where(diagonal(128), row, 0.0), axis=1, keepdims=True)


def fetch(sources, targets, sems):
    copies = [pltpu.make_async_copy(a, b, sems.at[i]) for i, (a, b) in enumerate(zip(sources, targets))]
    for copy in copies:
        copy.start()
    for copy in copies:
        copy.wait()


def pack_kernel(
    hidden_at, gain_at, a_query_at, a_value_at, value_up_at, grad_at, packet, hidden, gain, value_up, sems
):
    fetch(
        (hidden_at, gain_at, value_up_at, a_query_at, a_value_at, grad_at),
        (
            hidden,
            gain,
            value_up,
            packet.at[pl.ds(DOWNS_AT, RANK)],
            packet.at[pl.ds(DOWNS_AT + RANK, RANK)],
            packet.at[pl.ds(GRADS_AT, LENGTH)],
        ),
        sems,
    )
    values = hidden[...].astype(F32)
    packet[:LENGTH] = (values * gain[...].astype(F32)).astype(BF16)
    squares = jnp.sum(values * values, axis=1, keepdims=True)
    rows = jnp.concatenate([to_row(squares[:128]), to_row(squares[128:])], axis=0)
    high, low = two_terms(rows)
    packet[SQUARES_AT:COLUMNS_AT] = jnp.concatenate([high, low, jnp.zeros((12, 128), BF16)], axis=0)
    packet[COLUMNS_AT:GRADS_AT] = jnp.concatenate(
        [value_up[...], jnp.zeros((16, 128 - RANK), BF16)], axis=1
    )


def projection_kernel(place_ref, *rest):
    sources, out, held = rest[:4], rest[4], rest[5:9]
    q_levels, kv_levels, sems = rest[9:]
    half = pl.multiple_of(place_ref[0] * HALF, HALF)
    scales = pl.multiple_of(place_ref[0] * 128, 128)
    sources = (
        sources[0].at[pl.ds(half, HALF), :],
        sources[1].at[pl.ds(scales, 128), :],
        sources[2].at[:, pl.ds(half, HALF)],
        sources[3].at[:, pl.ds(scales, 128)],
    )
    fetch(sources, held, sems)
    wq, wq_scales, wkv, wkv_scales = held
    q_levels[...] = wq_scales[...].astype(F32)
    widen = lax.broadcasted_iota(jnp.int32, (32, 1024), 1) // 32 == lax.broadcasted_iota(
        jnp.int32, (32, 1024), 0
    )
    widen = jnp.where(widen, 1.0, 0.0).astype(BF16)
    for i in range(4):
        level = contract(wkv_scales[:, 32 * i : 32 * i + 32], widen, 1, 0)
        kv_levels[:, 1024 * i : 1024 * i + 1024] = level

    def step(j, carry):
        levels = q_levels[pl.ds(pl.multiple_of(j * 8, 8), 8), :]
        for e in range(2):
            rows = pl.ds(pl.multiple_of((2 * j + e) * 128, 128), 128)
            codes = wq[rows, :].astype(F32).reshape(4, 32, 128) * levels[4 * e : 4 * e + 4][:, None, :]
            out[rows, :] = codes.reshape(128, 128).astype(BF16)
            codes = wkv[:, rows].astype(F32) * kv_levels[:, rows]
            to = pl.multiple_of(HALF + (2 * j + e) * KV, KV)
            out[pl.ds(to, KV), :] = codes.astype(BF16)
        return carry

    lax.fori_loop(0, BLOCKS // 2, step, 0, unroll=2)


def output_kernel(place_ref, *rest):
    sources, out, (wo, wo_scales, sems) = rest[:2], rest[2], rest[3:]
    half = pl.ds(pl.multiple_of(place_ref[0] * HALF, HALF), HALF)
    fetch((sources[0].at[:, half], sources[1].at[:, half]), (wo, wo_scales), sems)

    def step(j, carry):
        block = pl.ds(pl.multiple_of(j * 128, 128), 128)
        level = wo_scales[:, block].astype(F32)
        codes = wo[:, block].astype(F32).reshape(4, 32, 128) * level[:, None, :]
        out[block, :] = codes.reshape(128, 128).astype(BF16)
        return carry

    lax.fori_loop(0, BLOCKS, step, 0, unroll=4)


def product_kernel(place_ref, *refs):
    sources, (kept, sent, box, value_up), held, sems = refs[:5], refs[5:9], refs[9:14], refs[14]
    copies = [pltpu.make_async_copy(a, b, sems.at[i]) for i, (a, b) in enumerate(zip(sources, held))]
    for copy in copies:
        copy.start()
    gathered, weights, outputs = held[0], held[1:3], held[3:5]

    def rows(start, number):
        return [gathered[b * PACKET + start : b * PACKET + start + number, :] for b in range(BLOCKS)]

    copies[0].wait()
    inputs = jnp.concatenate(rows(0, LENGTH), axis=1)
    low = contract(inputs, jnp.concatenate(rows(DOWNS_AT, 2 * RANK), axis=1), 1, 1)
    squares = sum(r.astype(F32) for r in rows(SQUARES_AT, 16))
    squares = squares[0:2] + squares[2:4]
    group = place_ref[1] // 4 * GROUP
    for i in range(GROUP):
        at = pl.multiple_of((group + i) * PACKET + COLUMNS_AT, 16)
        value_up[16 * i : 16 * i + 16, :] = gathered[pl.ds(at, 16), :]
    copies[1].wait()
    copies[2].wait()
    q = contract(inputs, jnp.concatenate([w[:HALF, :] for w in weights], axis=1), 1, 0)
    kv_weights = jnp.concatenate(
        [
            jnp.concatenate([w[HALF + b * KV : HALF + (b + 1) * KV, :] for b in range(BLOCKS)], axis=1)
            for w in weights
        ],
        axis=0,
    )
    kv = contract(kv_weights, inputs, 1, 1).astype(BF16)
    at_zero = place_ref[0] == 0
    for a in range(NX):
        mine = at_zero if a == 0 else jnp.logical_not(at_zero)
        whole = jnp.where(mine, kv[:KV], kv[KV:])
        whole = jnp.concatenate([whole[:, :128], whole[:, 128:]], axis=0)
        for i in range(GROUP):
            box[GROUP * a + i] = whole
    copies[3].wait()
    copies[4].wait()
    o_weights = jnp.concatenate(
        [
            jnp.concatenate([w[b * 128 : (b + 1) * 128, :] for b in range(BLOCKS)], axis=1)
            for w in outputs
        ],
        axis=0,
    )
    ctx = contract(jnp.concatenate(rows(GRADS_AT, LENGTH), axis=1), o_weights, 1, 1)
    high, rest = two_terms(squares)
    shared = jnp.concatenate([high.astype(F32), rest.astype(F32), jnp.zeros((12, 128), F32)], axis=0)
    for i, (out, cast) in enumerate(((kept, F32), (sent, BF16))):
        out[:LENGTH] = q[:, i * 128 : (i + 1) * 128].astype(cast)
        out[LENGTH:PER_HEAD] = ctx[:, i * 128 : (i + 1) * 128].astype(cast)
        out[PER_HEAD : PER_HEAD + LENGTH] = low.astype(cast)
        out[PER_HEAD + LENGTH :] = shared.astype(cast)


def turn(values, cosine, sine, axis):
    half = HEAD // 2
    if axis == 1:
        front, back = values[:, :half], values[:, half:]
    else:
        front, back = values[:half], values[half:]
    return jnp.concatenate([front * cosine - back * sine, back * cosine + front * sine], axis=axis)


def attention_kernel(
    kept,
    got,
    box,
    value_up_ref,
    hidden,
    gain,
    query_up,
    cosine,
    sine,
    cosine_t,
    sine_t,
    snapshot,
    out,
    up,
    normed,
):
    total = kept[...] + got[...].astype(F32)
    low = total[PER_HEAD : PER_HEAD + LENGTH]
    squares = total[PER_HEAD + LENGTH : PER_HEAD + LENGTH + 2]
    squares = squares + total[PER_HEAD + LENGTH + 2 : PER_HEAD + LENGTH + 4]
    inverse = lax.rsqrt(squares * (1.0 / FEATURES) + EPS)
    column = jnp.concatenate([to_column(inverse[0:1]), to_column(inverse[1:2])], axis=0)
    normed[...] = (hidden[...].astype(F32) * column * gain[...].astype(F32)).astype(BF16)
    lows = (low * column).astype(BF16)
    linear = total[:LENGTH] * column + ADAPTER_SCALE * contract(lows[:, :RANK], query_up[...], 1, 0)
    queries = turn(linear, cosine[...], sine[...], 1).astype(BF16)
    grads = total[LENGTH:PER_HEAD].astype(BF16)
    row_inverse = jnp.concatenate([inverse[0:1], inverse[1:2]], axis=1)
    value_up = value_up_ref[:, :RANK]

    def side(start):
        rows = []
        for i in range(start, start + GROUP // 2):
            part = sum(box[GROUP * a + i].astype(F32) for a in range(NX))
            rows.append(jnp.concatenate([part[:KV], part[KV:]], axis=1))
        return jnp.concatenate(rows, axis=0) * row_inverse

    keys = side(0).astype(BF16).astype(F32)
    keys = turn(keys, cosine_t[...], sine_t[...], 0).astype(BF16)
    values = (side(GROUP // 2) + ADAPTER_SCALE * contract(value_up, lows[:, RANK:], 1, 1)).astype(BF16)
    scale = HEAD ** (-0.5)
    scores = contract(queries, keys, 1, 0) * scale
    row = lax.broadcasted_iota(jnp.int32, (LENGTH, LENGTH), 0)
    column = lax.broadcasted_iota(jnp.int32, (LENGTH, LENGTH), 1)
    segment = snapshot[...].astype(F32)
    own = jnp.concatenate([to_column(segment[:, :128]), to_column(segment[:, 128:])], axis=0)
    allowed = jnp.logical_and(column <= row, own == segment)
    scores = jnp.where(allowed, scores, MASKED)
    weights = jnp.exp(scores - jnp.max(scores, axis=1, keepdims=True))
    prob = weights / jnp.sum(weights, axis=1, keepdims=True)
    grad_prob = contract(grads, values, 1, 0)
    grad_value = contract(prob.astype(BF16), grads, 0, 0).astype(BF16)
    inner = jnp.sum(prob * grad_prob, axis=1, keepdims=True)
    grad_score = (prob * (grad_prob - inner)).astype(BF16)
    grad_query = contract(grad_score, keys, 1, 1) * scale
    grad_linear = turn(grad_query, cosine[...], -sine[...], 1).astype(BF16)
    low_q, low_v = lows[:, :RANK], lows[:, RANK:]
    up[...] = ADAPTER_SCALE * contract(low_q, grad_linear, 0, 0)
    slices = ADAPTER_SCALE * contract(grad_value, low_v, 0, 0)
    slices = jnp.concatenate([slices, jnp.zeros((HEAD, 128 - RANK), F32)], axis=1).astype(BF16)
    grad_low = jnp.concatenate(
        [
            ADAPTER_SCALE * contract(grad_linear, query_up[...], 1, 1),
            ADAPTER_SCALE * contract(grad_value, value_up, 1, 0),
        ],
        axis=1,
    ).astype(BF16)
    rows = LENGTH // GROUP
    for i in range(GROUP):
        out[i, :rows, :] = grad_low[i * rows : (i + 1) * rows]
        out[i, rows:, :] = slices[16 * i : 16 * i + 16]


def near_kernel(parts, low, value):
    total = jnp.sum(parts[...].astype(F32), axis=0)
    rows = LENGTH // GROUP
    value[...] = total[rows:]
    for i in range(8):
        low[i] = total[:rows].astype(BF16)


def far_kernel(parts, low):
    total = jnp.sum(parts[...].astype(F32), axis=0).astype(BF16)
    for i in range(GROUP):
        low[i] = total


def rows_kernel(normed, low, up, value, out):
    whole = jnp.concatenate([low[i] for i in range(GROUP)], axis=0)
    rows = contract(normed[...], whole, 0, 0).astype(BF16)
    last = jnp.concatenate([up[...], value[...]], axis=0).astype(BF16)
    for i in range(8):
        out[i, :HEAD, :] = rows
        out[i, HEAD:, :] = last


def total_kernel(parts, grad_a_query, query_up, grad_a_value, value):
    total = jnp.sum(parts[...].astype(F32), axis=0)
    rows = total[:HEAD].T
    grad_a_query[...] = rows[:RANK]
    grad_a_value[...] = rows[RANK:]
    query_up[...] = total[HEAD : HEAD + RANK]
    value[...] = total[HEAD + RANK :, :RANK]


def local(
    hidden_in,
    out_grad,
    snapshot_ids,
    norm_gain,
    wq_codes,
    wq_scales,
    wkv_codes,
    wkv_scales,
    wo_codes,
    wo_scales,
    a_query,
    query_up_weight,
    a_value,
    value_up_weight,
):
    head_index = lax.axis_index("fsdp")
    spot = jnp.stack([head_index // (NZ * NC), head_index // NC % NZ, head_index % NC]).astype(jnp.int32)
    gain = norm_gain[None, :]

    packet = call(
        pack_kernel,
        shape(PACKET, 128),
        hidden_in,
        gain,
        a_query,
        a_value,
        value_up_weight.T,
        out_grad,
        scratch=[
            pltpu.VMEM((LENGTH, 128), BF16),
            pltpu.VMEM((1, 128), BF16),
            pltpu.VMEM((16, RANK), BF16),
            pltpu.SemaphoreType.DMA((6,)),
        ],
        megabytes=56,
        held=True,
    )
    gathered = lax.all_gather(packet, "fsdp", axis=0, tiled=True, axis_index_groups=HALF_GROUPS)

    def projection(spot):
        return call(
            projection_kernel,
            shape(BLOCKS * (128 + KV), 128),
            spot,
            wq_codes,
            wq_scales,
            wkv_codes.T,
            wkv_scales.T,
            scratch=[
                pltpu.VMEM((HALF, 128), BF16),
                pltpu.VMEM((128, 128), BF16),
                pltpu.VMEM((KV, HALF), BF16),
                pltpu.VMEM((KV, 128), BF16),
                pltpu.VMEM((128, 128), F32),
                pltpu.VMEM((KV, HALF), F32),
                pltpu.SemaphoreType.DMA((4,)),
            ],
            megabytes=56,
            held=True,
        )

    def output(spot):
        return call(
            output_kernel,
            shape(BLOCKS * 128, 128),
            spot,
            wo_codes,
            wo_scales,
            scratch=[
                pltpu.VMEM((128, HALF), BF16),
                pltpu.VMEM((4, HALF), BF16),
                pltpu.SemaphoreType.DMA((2,)),
            ],
            megabytes=56,
            held=True,
        )

    other = spot ^ jnp.array([1, 0, 0], jnp.int32)
    sent_projection = projection(after(other, packet))
    sent_output = output(after(other, sent_projection))
    own_projection = projection(after(spot, sent_output))
    own_output = output(after(spot, own_projection))
    got_projection = swap_weights(sent_projection, NZ * NC)
    got_output = swap_weights(sent_output, NZ * NC)

    rows = PER_HEAD + SHARED
    kept, sent, box, value_up = call(
        product_kernel,
        [
            shape(rows, 128, dtype=F32),
            shape(rows, 128),
            shape(2 * GROUP, 2 * KV, 128),
            shape(128, 128),
        ],
        spot,
        gathered,
        own_projection,
        got_projection,
        own_output,
        got_output,
        scratch=[
            pltpu.VMEM((BLOCKS * PACKET, 128), BF16),
            *[pltpu.VMEM((BLOCKS * (128 + KV), 128), BF16)] * 2,
            *[pltpu.VMEM((BLOCKS * 128, 128), BF16)] * 2,
            pltpu.SemaphoreType.DMA((5,)),
        ],
        megabytes=56,
        held=True,
    )
    got = swap(sent, NZ * NC)
    box = exchange(box, "fsdp", BOX_GROUPS)

    cosine, sine = rope_tables()
    slices, up, normed = call(
        attention_kernel,
        [shape(GROUP, LENGTH // GROUP + 16, 128), shape(RANK, HEAD, dtype=F32), shape(LENGTH, 128)],
        kept,
        got,
        box,
        value_up,
        hidden_in,
        gain,
        query_up_weight,
        jnp.asarray(cosine),
        jnp.asarray(sine),
        jnp.asarray(cosine.T.copy()),
        jnp.asarray(sine.T.copy()),
        snapshot_ids,
    )

    low, value = call(
        near_kernel,
        [shape(8, LENGTH // GROUP, 128), shape(16, 128, dtype=F32)],
        exchange(slices, "fsdp", NEAR_GROUPS),
    )
    low = call(far_kernel, shape(GROUP, LENGTH // GROUP, 128), exchange(low, "fsdp", FAR_GROUPS))
    mine = call(
        rows_kernel,
        shape(8, HEAD + RANK + 16, 128),
        normed,
        exchange(low, "fsdp", NEAR_GROUPS),
        up,
        value,
    )
    grad_a_query, query_up, grad_a_value, value = call(
        total_kernel,
        [
            shape(RANK, HEAD, dtype=F32),
            shape(RANK, HEAD, dtype=F32),
            shape(RANK, HEAD, dtype=F32),
            shape(16, RANK, dtype=F32),
        ],
        exchange(mine, "dp"),
    )
    return grad_a_query.T, query_up, grad_a_value.T, value.T


def solution(mesh):
    in_specs = (
        P("dp", "fsdp"),
        P("dp", "fsdp"),
        P("dp", None),
        P("fsdp"),
        P(None, "fsdp"),
        P(None, "fsdp"),
        P(None, "fsdp"),
        P(None, "fsdp"),
        P("fsdp", None),
        P("fsdp", None),
        P(None, "fsdp"),
        P(None, "fsdp"),
        P(None, "fsdp"),
        P(None, "fsdp"),
    )
    out_specs = (P("fsdp", None), P(None, "fsdp"), P("fsdp", None), P(None, "fsdp"))
    return jax.shard_map(local, mesh=mesh, in_specs=in_specs, out_specs=out_specs, check_vma=False)
```

```python
import math

import jax
import jax.numpy as jnp
import numpy as np
from jax import lax
from jax.experimental import pallas as pl
from jax.experimental.pallas import tpu as pltpu
from jax.sharding import PartitionSpec as P

GROUP = 8
EPS = 1e-05
ADAPTER_SCALE = 0.5
ROPE_BASE = 500000.0
MASKED = -1e30

NX, NZ, NC = 2, 16, 2
LENGTH, HEAD, RANK, KV = 256, 128, 64, 32
FEATURES = NX * NZ * NC * HEAD
HALF = FEATURES // NX
BLOCKS = NZ * NC
DOWNS_AT = LENGTH
SQUARES_AT = DOWNS_AT + 2 * RANK
COLUMNS_AT = SQUARES_AT + 16
GRADS_AT = COLUMNS_AT + 16
PACKET = GRADS_AT + LENGTH
PER_HEAD = 2 * LENGTH
SHARED = LENGTH + 16

F32, BF16 = jnp.float32, jnp.bfloat16
VMEM = pl.BlockSpec(memory_space=pltpu.VMEM)
SMEM = pl.BlockSpec(memory_space=pltpu.SMEM)


def place(a, z, c):
    return a * (NZ * NC) + z * NC + c


HALF_GROUPS = [[place(a, z, c) for z in range(NZ) for c in range(NC)] for a in range(NX)]
BOX_GROUPS = [
    [place(a, 4 * b + i, c) for a in range(NX) for i in range(4) for c in range(NC)] for b in range(4)
]
NEAR_GROUPS = [[GROUP * g + i for i in range(GROUP)][::-1] for g in range(8)]
FAR_GROUPS = [
    [place(a, z + 4 * k, c) for a in range(NX) for k in (2, 3, 0, 1)] for z in range(4) for c in range(NC)
]


def swap(value, mask):
    return lax.ppermute(value, "fsdp", [(i, i ^ mask) for i in range(NX * NZ * NC)])


def swap_weights(value, mask):
    if mask < NZ * NC:
        return swap(value, mask)
    size = NX * NZ * NC
    rows = lax.axis_size("dp")
    pairs = [(d * size + i, (d ^ 1) * size + (i ^ mask)) for d in range(rows) for i in range(size)]
    return lax.ppermute(value, ("dp", "fsdp"), pairs)


def exchange(value, axis, groups=None):
    return lax.all_to_all(value, axis, 0, 0, axis_index_groups=groups)


def after(value, *others):
    return lax.optimization_barrier((value, *others))[0]


def rope_tables():
    positions = np.arange(LENGTH, dtype=np.float32)[:, None]
    steps = np.arange(HEAD // 2, dtype=np.float32)
    frequency = np.exp(steps * np.float32(-2.0 * math.log(ROPE_BASE) / HEAD)).astype(np.float32)
    angles = positions * frequency[None, :]
    return np.cos(angles).astype(np.float32), np.sin(angles).astype(np.float32)


def contract(left_arr, right_arr, left_dim, right_dim):
    return lax.dot_general(
        left_arr,
        right_arr,
        (((left_dim,), (right_dim,)), ((), ())),
        preferred_element_type=F32,
    )


def two_terms(value):
    high = value.astype(BF16)
    return high, (value - high.astype(F32)).astype(BF16)


def call(body, outs, *operands, scratch=(), megabytes=32, held=False):
    specs = [SMEM if o.dtype == jnp.int32 and o.ndim == 1 else VMEM for o in operands]
    if held is not False:
        here = range(len(operands)) if held is True else held
        specs = [
            pl.BlockSpec(memory_space=pl.ANY) if i in here and spec is not SMEM else spec
            for i, spec in enumerate(specs)
        ]
    many = isinstance(outs, (list, tuple))
    return pl.pallas_call(
        body,
        out_shape=outs,
        in_specs=specs,
        out_specs=[VMEM] * len(outs) if many else VMEM,
        scratch_shapes=list(scratch),
        compiler_params=pltpu.CompilerParams(vmem_limit_bytes=megabytes << 20),
    )(*operands)


def shape(*dims, dtype=BF16):
    return jax.ShapeDtypeStruct(dims, dtype)


def diagonal(size):
    return lax.broadcasted_iota(jnp.int32, (size, size), 0) == lax.broadcasted_iota(
        jnp.int32, (size, size), 1
    )


def to_row(column):
    return jnp.sum(jnp.where(diagonal(128), column, 0.0), axis=0, keepdims=True)


def to_column(row):
    return jnp.sum(jnp.where(diagonal(128), row, 0.0), axis=1, keepdims=True)


def fetch(sources, targets, sems):
    copies = [pltpu.make_async_copy(a, b, sems.at[i]) for i, (a, b) in enumerate(zip(sources, targets))]
    for copy in copies:
        copy.start()
    for copy in copies:
        copy.wait()


def pack_kernel(
    hidden_at, gain_at, a_query_at, a_value_at, value_up_at, grad_at, packet, hidden, gain, value_up, sems
):
    fetch(
        (hidden_at, gain_at, value_up_at, a_query_at, a_value_at, grad_at),
        (
            hidden,
            gain,
            value_up,
            packet.at[pl.ds(DOWNS_AT, RANK)],
            packet.at[pl.ds(DOWNS_AT + RANK, RANK)],
            packet.at[pl.ds(GRADS_AT, LENGTH)],
        ),
        sems,
    )
    values = hidden[...].astype(F32)
    packet[:LENGTH] = (values * gain[...].astype(F32)).astype(BF16)
    squares = jnp.sum(values * values, axis=1, keepdims=True)
    rows = jnp.concatenate([to_row(squares[:128]), to_row(squares[128:])], axis=0)
    high, low = two_terms(rows)
    packet[SQUARES_AT:COLUMNS_AT] = jnp.concatenate([high, low, jnp.zeros((12, 128), BF16)], axis=0)
    packet[COLUMNS_AT:GRADS_AT] = jnp.concatenate(
        [value_up[...], jnp.zeros((16, 128 - RANK), BF16)], axis=1
    )


def projection_kernel(place_ref, *rest):
    sources, out, held = rest[:4], rest[4], rest[5:9]
    q_levels, kv_levels, sems = rest[9:]
    half = pl.multiple_of(place_ref[0] * HALF, HALF)
    scales = pl.multiple_of(place_ref[0] * 128, 128)
    sources = (
        sources[0].at[pl.ds(half, HALF), :],
        sources[1].at[pl.ds(scales, 128), :],
        sources[2].at[:, pl.ds(half, HALF)],
        sources[3].at[:, pl.ds(scales, 128)],
    )
    fetch(sources, held, sems)
    wq, wq_scales, wkv, wkv_scales = held
    q_levels[...] = wq_scales[...].astype(F32)
    widen = lax.broadcasted_iota(jnp.int32, (32, 1024), 1) // 32 == lax.broadcasted_iota(
        jnp.int32, (32, 1024), 0
    )
    widen = jnp.where(widen, 1.0, 0.0).astype(BF16)
    for i in range(4):
        level = contract(wkv_scales[:, 32 * i : 32 * i + 32], widen, 1, 0)
        kv_levels[:, 1024 * i : 1024 * i + 1024] = level

    def step(j, carry):
        levels = q_levels[pl.ds(pl.multiple_of(j * 8, 8), 8), :]
        for e in range(2):
            rows = pl.ds(pl.multiple_of((2 * j + e) * 128, 128), 128)
            codes = wq[rows, :].astype(F32).reshape(4, 32, 128) * levels[4 * e : 4 * e + 4][:, None, :]
            out[rows, :] = codes.reshape(128, 128).astype(BF16)
            codes = wkv[:, rows].astype(F32) * kv_levels[:, rows]
            to = pl.multiple_of(HALF + (2 * j + e) * KV, KV)
            out[pl.ds(to, KV), :] = codes.astype(BF16)
        return carry

    lax.fori_loop(0, BLOCKS // 2, step, 0, unroll=2)


def output_kernel(place_ref, *rest):
    sources, out, (wo, wo_scales, sems) = rest[:2], rest[2], rest[3:]
    half = pl.ds(pl.multiple_of(place_ref[0] * HALF, HALF), HALF)
    fetch((sources[0].at[:, half], sources[1].at[:, half]), (wo, wo_scales), sems)

    def step(j, carry):
        block = pl.ds(pl.multiple_of(j * 128, 128), 128)
        level = wo_scales[:, block].astype(F32)
        codes = wo[:, block].astype(F32).reshape(4, 32, 128) * level[:, None, :]
        out[block, :] = codes.reshape(128, 128).astype(BF16)
        return carry

    lax.fori_loop(0, BLOCKS, step, 0, unroll=4)


def product_kernel(place_ref, gathered_at, *refs):
    weights, outputs, (kept, sent, box, value_up), gathered, sems = refs[:2], refs[2:4], refs[4:8], refs[8], refs[9]

    def start(source, target, i):
        copy = pltpu.make_async_copy(source, target, sems.at[i])
        copy.start()
        return copy

    def part(first, number):
        return pl.ds(0, BLOCKS), pl.ds(first, number), slice(None)

    x_copy = start(gathered_at.at[part(0, LENGTH)], gathered.at[part(0, LENGTH)], 0)
    rest = part(LENGTH, GRADS_AT - LENGTH)
    a_copy = start(gathered_at.at[rest], gathered.at[rest], 1)
    g_copy = start(gathered_at.at[part(GRADS_AT, LENGTH)], gathered.at[part(GRADS_AT, LENGTH)], 2)

    def rows(first, number):
        return [gathered[b, first : first + number, :] for b in range(BLOCKS)]

    x_copy.wait()
    inputs = jnp.concatenate(rows(0, LENGTH), axis=1)
    q = contract(inputs, jnp.concatenate([w[:HALF, :] for w in weights], axis=1), 1, 0)
    a_copy.wait()
    narrow = [jnp.concatenate(rows(DOWNS_AT, 2 * RANK), axis=1)]
    for w in weights:
        narrow.append(
            jnp.concatenate([w[HALF + b * KV : HALF + (b + 1) * KV, :] for b in range(BLOCKS)], axis=1)
        )
    narrow = contract(inputs, jnp.concatenate(narrow, axis=0), 1, 1)
    low, kv = narrow[:, : 2 * RANK], narrow[:, 2 * RANK :].T.astype(BF16)
    at_zero = place_ref[0] == 0
    for a in range(NX):
        mine = at_zero if a == 0 else jnp.logical_not(at_zero)
        whole = jnp.where(mine, kv[:KV], kv[KV:])
        whole = jnp.concatenate([whole[:, :128], whole[:, 128:]], axis=0)
        for i in range(GROUP):
            box[GROUP * a + i] = whole
    squares = sum(r.astype(F32) for r in rows(SQUARES_AT, 16))
    squares = squares[0:2] + squares[2:4]
    group = place_ref[1] // 4 * GROUP
    for i in range(GROUP):
        value_up[16 * i : 16 * i + 16, :] = gathered[group + i, COLUMNS_AT:GRADS_AT, :]
    g_copy.wait()
    o_weights = jnp.concatenate(
        [
            jnp.concatenate([w[b * 128 : (b + 1) * 128, :] for b in range(BLOCKS)], axis=1)
            for w in outputs
        ],
        axis=0,
    )
    ctx = contract(jnp.concatenate(rows(GRADS_AT, LENGTH), axis=1), o_weights, 1, 1)
    high, rest = two_terms(squares)
    shared = jnp.concatenate([high.astype(F32), rest.astype(F32), jnp.zeros((12, 128), F32)], axis=0)
    for i, (out, cast) in enumerate(((kept, F32), (sent, BF16))):
        out[:LENGTH] = q[:, i * 128 : (i + 1) * 128].astype(cast)
        out[LENGTH:PER_HEAD] = ctx[:, i * 128 : (i + 1) * 128].astype(cast)
        out[PER_HEAD : PER_HEAD + LENGTH] = low.astype(cast)
        out[PER_HEAD + LENGTH :] = shared.astype(cast)


def turn(values, cosine, sine, axis):
    half = HEAD // 2
    if axis == 1:
        front, back = values[:, :half], values[:, half:]
    else:
        front, back = values[:half], values[half:]
    return jnp.concatenate([front * cosine - back * sine, back * cosine + front * sine], axis=axis)


def attention_kernel(
    kept,
    got,
    box,
    value_up_ref,
    hidden,
    gain,
    query_up,
    cosine,
    sine,
    cosine_t,
    sine_t,
    snapshot,
    out,
    up,
    normed,
):
    total = kept[...] + got[...].astype(F32)
    low = total[PER_HEAD : PER_HEAD + LENGTH]
    squares = total[PER_HEAD + LENGTH : PER_HEAD + LENGTH + 2]
    squares = squares + total[PER_HEAD + LENGTH + 2 : PER_HEAD + LENGTH + 4]
    inverse = lax.rsqrt(squares * (1.0 / FEATURES) + EPS)
    column = jnp.concatenate([to_column(inverse[0:1]), to_column(inverse[1:2])], axis=0)
    normed[...] = (hidden[...].astype(F32) * column * gain[...].astype(F32)).astype(BF16)
    lows = (low * column).astype(BF16)
    linear = total[:LENGTH] * column + ADAPTER_SCALE * contract(lows[:, :RANK], query_up[...], 1, 0)
    queries = turn(linear, cosine[...], sine[...], 1).astype(BF16)
    grads = total[LENGTH:PER_HEAD].astype(BF16)
    row_inverse = jnp.concatenate([inverse[0:1], inverse[1:2]], axis=1)
    value_up = value_up_ref[:, :RANK]

    def side(start):
        rows = []
        for i in range(start, start + GROUP // 2):
            part = sum(box[GROUP * a + i].astype(F32) for a in range(NX))
            rows.append(jnp.concatenate([part[:KV], part[KV:]], axis=1))
        return jnp.concatenate(rows, axis=0) * row_inverse

    keys = side(0).astype(BF16).astype(F32)
    keys = turn(keys, cosine_t[...], sine_t[...], 0).astype(BF16)
    values = (side(GROUP // 2) + ADAPTER_SCALE * contract(value_up, lows[:, RANK:], 1, 1)).astype(BF16)
    scale = HEAD ** (-0.5)
    scores = contract(queries, keys, 1, 0) * scale
    row = lax.broadcasted_iota(jnp.int32, (LENGTH, LENGTH), 0)
    column = lax.broadcasted_iota(jnp.int32, (LENGTH, LENGTH), 1)
    segment = snapshot[...].astype(F32)
    own = jnp.concatenate([to_column(segment[:, :128]), to_column(segment[:, 128:])], axis=0)
    allowed = jnp.logical_and(column <= row, own == segment)
    scores = jnp.where(allowed, scores, MASKED)
    weights = jnp.exp(scores - jnp.max(scores, axis=1, keepdims=True))
    prob = weights / jnp.sum(weights, axis=1, keepdims=True)
    grad_prob = contract(grads, values, 1, 0)
    grad_value = contract(prob.astype(BF16), grads, 0, 0).astype(BF16)
    inner = jnp.sum(prob * grad_prob, axis=1, keepdims=True)
    grad_score = (prob * (grad_prob - inner)).astype(BF16)
    grad_query = contract(grad_score, keys, 1, 1) * scale
    grad_linear = turn(grad_query, cosine[...], -sine[...], 1).astype(BF16)
    low_q, low_v = lows[:, :RANK], lows[:, RANK:]
    up[...] = ADAPTER_SCALE * contract(low_q, grad_linear, 0, 0)
    slices = ADAPTER_SCALE * contract(grad_value, low_v, 0, 0)
    slices = jnp.concatenate([slices, jnp.zeros((HEAD, 128 - RANK), F32)], axis=1).astype(BF16)
    grad_low = jnp.concatenate(
        [
            ADAPTER_SCALE * contract(grad_linear, query_up[...], 1, 1),
            ADAPTER_SCALE * contract(grad_value, value_up, 1, 0),
        ],
        axis=1,
    ).astype(BF16)
    rows = LENGTH // GROUP
    for i in range(GROUP):
        out[GROUP - 1 - i, :rows, :] = grad_low[i * rows : (i + 1) * rows]
        out[GROUP - 1 - i, rows:, :] = slices[16 * i : 16 * i + 16]


def near_kernel(parts, low, value):
    total = jnp.sum(parts[...].astype(F32), axis=0)
    rows = LENGTH // GROUP
    value[...] = total[rows:]
    for i in range(8):
        low[i] = total[:rows].astype(BF16)


def far_kernel(parts, low):
    total = jnp.sum(parts[...].astype(F32), axis=0).astype(BF16)
    for i in range(GROUP):
        low[i] = total


def rows_kernel(normed, low, up, value, out):
    whole = jnp.concatenate([low[GROUP - 1 - i] for i in range(GROUP)], axis=0)
    rows = contract(normed[...], whole, 0, 0).astype(BF16)
    last = jnp.concatenate([up[...], value[...]], axis=0).astype(BF16)
    for i in range(8):
        out[i, :HEAD, :] = rows
        out[i, HEAD:, :] = last


def total_kernel(parts, grad_a_query, query_up, grad_a_value, value):
    total = jnp.sum(parts[...].astype(F32), axis=0)
    rows = total[:HEAD].T
    grad_a_query[...] = rows[:RANK]
    grad_a_value[...] = rows[RANK:]
    query_up[...] = total[HEAD : HEAD + RANK]
    value[...] = total[HEAD + RANK :, :RANK]


def local(
    hidden_in,
    out_grad,
    snapshot_ids,
    norm_gain,
    wq_codes,
    wq_scales,
    wkv_codes,
    wkv_scales,
    wo_codes,
    wo_scales,
    a_query,
    query_up_weight,
    a_value,
    value_up_weight,
):
    head_index = lax.axis_index("fsdp")
    spot = jnp.stack([head_index // (NZ * NC), head_index // NC % NZ, head_index % NC]).astype(jnp.int32)
    gain = norm_gain[None, :]

    packet = call(
        pack_kernel,
        shape(PACKET, 128),
        hidden_in,
        gain,
        a_query,
        a_value,
        value_up_weight.T,
        out_grad,
        scratch=[
            pltpu.VMEM((LENGTH, 128), BF16),
            pltpu.VMEM((1, 128), BF16),
            pltpu.VMEM((16, RANK), BF16),
            pltpu.SemaphoreType.DMA((6,)),
        ],
        megabytes=56,
        held=True,
    )
    gathered = lax.all_gather(packet, "fsdp", axis=0, tiled=True, axis_index_groups=HALF_GROUPS)

    def projection(spot):
        return call(
            projection_kernel,
            shape(BLOCKS * (128 + KV), 128),
            spot,
            wq_codes,
            wq_scales,
            wkv_codes.T,
            wkv_scales.T,
            scratch=[
                pltpu.VMEM((HALF, 128), BF16),
                pltpu.VMEM((128, 128), BF16),
                pltpu.VMEM((KV, HALF), BF16),
                pltpu.VMEM((KV, 128), BF16),
                pltpu.VMEM((128, 128), F32),
                pltpu.VMEM((KV, HALF), F32),
                pltpu.SemaphoreType.DMA((4,)),
            ],
            megabytes=12,
            held=True,
        )

    def output(spot):
        return call(
            output_kernel,
            shape(BLOCKS * 128, 128),
            spot,
            wo_codes,
            wo_scales,
            scratch=[
                pltpu.VMEM((128, HALF), BF16),
                pltpu.VMEM((4, HALF), BF16),
                pltpu.SemaphoreType.DMA((2,)),
            ],
            megabytes=12,
            held=True,
        )

    other = spot ^ jnp.array([1, 0, 0], jnp.int32)
    sent_projection = projection(after(other, packet))
    sent_output = output(after(other, sent_projection))
    own_projection = projection(after(spot, sent_output))
    own_output = output(after(spot, own_projection))
    got_projection = swap_weights(sent_projection, NZ * NC)
    got_output = swap_weights(sent_output, NZ * NC)

    rows = PER_HEAD + SHARED
    gathered = gathered.reshape(BLOCKS, PACKET, 128)
    kept, sent, box, value_up = call(
        product_kernel,
        [
            shape(rows, 128, dtype=F32),
            shape(rows, 128),
            shape(2 * GROUP, 2 * KV, 128),
            shape(128, 128),
        ],
        spot,
        gathered,
        own_projection,
        got_projection,
        own_output,
        got_output,
        scratch=[
            pltpu.VMEM((BLOCKS, PACKET, 128), BF16),
            pltpu.SemaphoreType.DMA((3,)),
        ],
        megabytes=50,
        held=(1,),
    )
    got = swap(sent, NZ * NC)
    box = exchange(box, "fsdp", BOX_GROUPS)

    cosine, sine = rope_tables()
    slices, up, normed = call(
        attention_kernel,
        [shape(GROUP, LENGTH // GROUP + 16, 128), shape(RANK, HEAD, dtype=F32), shape(LENGTH, 128)],
        kept,
        got,
        box,
        value_up,
        hidden_in,
        gain,
        query_up_weight,
        jnp.asarray(cosine),
        jnp.asarray(sine),
        jnp.asarray(cosine.T.copy()),
        jnp.asarray(sine.T.copy()),
        snapshot_ids,
    )

    low, value = call(
        near_kernel,
        [shape(8, LENGTH // GROUP, 128), shape(16, 128, dtype=F32)],
        exchange(slices, "fsdp", NEAR_GROUPS),
    )
    low = call(far_kernel, shape(GROUP, LENGTH // GROUP, 128), exchange(low, "fsdp", FAR_GROUPS))
    mine = call(
        rows_kernel,
        shape(8, HEAD + RANK + 16, 128),
        normed,
        exchange(low, "fsdp", NEAR_GROUPS),
        up,
        value,
    )
    grad_a_query, query_up, grad_a_value, value = call(
        total_kernel,
        [
            shape(RANK, HEAD, dtype=F32),
            shape(RANK, HEAD, dtype=F32),
            shape(RANK, HEAD, dtype=F32),
            shape(16, RANK, dtype=F32),
        ],
        exchange(mine, "dp", [list(range(7, -1, -1))]),
    )
    return grad_a_query.T, query_up, grad_a_value.T, value.T


def solution(mesh):
    in_specs = (
        P("dp", "fsdp"),
        P("dp", "fsdp"),
        P("dp", None),
        P("fsdp"),
        P(None, "fsdp"),
        P(None, "fsdp"),
        P(None, "fsdp"),
        P(None, "fsdp"),
        P("fsdp", None),
        P("fsdp", None),
        P(None, "fsdp"),
        P(None, "fsdp"),
        P(None, "fsdp"),
        P(None, "fsdp"),
    )
    out_specs = (P("fsdp", None), P(None, "fsdp"), P("fsdp", None), P(None, "fsdp"))
    return jax.shard_map(local, mesh=mesh, in_specs=in_specs, out_specs=out_specs, check_vma=False)
```

```python
import math

import jax
import jax.numpy as jnp
import numpy as np
from jax import lax
from jax.experimental import pallas as pl
from jax.experimental.pallas import tpu as pltpu
from jax.sharding import PartitionSpec as P

GROUP = 8
EPS = 1e-05
ADAPTER_SCALE = 0.5
ROPE_BASE = 500000.0
MASKED = -1e30

NX, NZ, NC = 2, 16, 2
LENGTH, HEAD, RANK, KV = 256, 128, 64, 32
FEATURES = NX * NZ * NC * HEAD
HALF = FEATURES // NX
PARTS = 8
BLOCKS = NZ * NC
DOWNS_AT = LENGTH
SQUARES_AT = DOWNS_AT + 2 * RANK
COLUMNS_AT = SQUARES_AT + 16
GRADS_AT = COLUMNS_AT + 16
PACKET = GRADS_AT + LENGTH
PER_HEAD = 2 * LENGTH
SHARED = LENGTH + 16

F32, BF16 = jnp.float32, jnp.bfloat16
VMEM = pl.BlockSpec(memory_space=pltpu.VMEM)
SMEM = pl.BlockSpec(memory_space=pltpu.SMEM)


def place(a, z, c):
    return a * (NZ * NC) + z * NC + c


HALF_GROUPS = [[place(a, z, c) for z in range(NZ) for c in range(NC)] for a in range(NX)]
BOX_GROUPS = [
    [place(a, 4 * b + i, c) for a in range(NX) for i in range(4) for c in range(NC)] for b in range(4)
]
NEAR_GROUPS = [[GROUP * g + i for i in range(GROUP)][::-1] for g in range(8)]
FAR_GROUPS = [
    [place(a, z + 4 * k, c) for a in range(NX) for k in (2, 3, 0, 1)] for z in range(4) for c in range(NC)
]


def swap(value, mask):
    return lax.ppermute(value, "fsdp", [(i, i ^ mask) for i in range(NX * NZ * NC)])


def swap_weights(value, mask):
    if mask < NZ * NC:
        return swap(value, mask)
    size = NX * NZ * NC
    rows = lax.axis_size("dp")
    pairs = [(d * size + i, (d ^ 1) * size + (i ^ mask)) for d in range(rows) for i in range(size)]
    return lax.ppermute(value, ("dp", "fsdp"), pairs)


def exchange(value, axis, groups=None):
    return lax.all_to_all(value, axis, 0, 0, axis_index_groups=groups)


def after(value, *others):
    return lax.optimization_barrier((value, *others))[0]


def rope_tables():
    positions = np.arange(LENGTH, dtype=np.float32)[:, None]
    steps = np.arange(HEAD // 2, dtype=np.float32)
    frequency = np.exp(steps * np.float32(-2.0 * math.log(ROPE_BASE) / HEAD)).astype(np.float32)
    angles = positions * frequency[None, :]
    return np.cos(angles).astype(np.float32), np.sin(angles).astype(np.float32)


def contract(left_arr, right_arr, left_dim, right_dim):
    return lax.dot_general(
        left_arr,
        right_arr,
        (((left_dim,), (right_dim,)), ((), ())),
        preferred_element_type=F32,
    )


def two_terms(value):
    high = value.astype(BF16)
    return high, (value - high.astype(F32)).astype(BF16)


def call(body, outs, *operands, scratch=(), megabytes=32, held=False):
    specs = [SMEM if o.dtype == jnp.int32 and o.ndim == 1 else VMEM for o in operands]
    if held is not False:
        here = range(len(operands)) if held is True else held
        specs = [
            pl.BlockSpec(memory_space=pl.ANY) if i in here and spec is not SMEM else spec
            for i, spec in enumerate(specs)
        ]
    many = isinstance(outs, (list, tuple))
    return pl.pallas_call(
        body,
        out_shape=outs,
        in_specs=specs,
        out_specs=[VMEM] * len(outs) if many else VMEM,
        scratch_shapes=list(scratch),
        compiler_params=pltpu.CompilerParams(vmem_limit_bytes=megabytes << 20),
    )(*operands)


def shape(*dims, dtype=BF16):
    return jax.ShapeDtypeStruct(dims, dtype)


def diagonal(size):
    return lax.broadcasted_iota(jnp.int32, (size, size), 0) == lax.broadcasted_iota(
        jnp.int32, (size, size), 1
    )


def to_row(column):
    return jnp.sum(jnp.where(diagonal(128), column, 0.0), axis=0, keepdims=True)


def to_column(row):
    return jnp.sum(jnp.where(diagonal(128), row, 0.0), axis=1, keepdims=True)


def fetch(sources, targets, sems):
    copies = [pltpu.make_async_copy(a, b, sems.at[i]) for i, (a, b) in enumerate(zip(sources, targets))]
    for copy in copies:
        copy.start()
    for copy in copies:
        copy.wait()


def pack_kernel(
    hidden_at, gain_at, a_query_at, a_value_at, value_up_at, grad_at, packet, hidden, gain, value_up, sems
):
    fetch(
        (hidden_at, gain_at, value_up_at, a_query_at, a_value_at, grad_at),
        (
            hidden,
            gain,
            value_up,
            packet.at[pl.ds(DOWNS_AT, RANK)],
            packet.at[pl.ds(DOWNS_AT + RANK, RANK)],
            packet.at[pl.ds(GRADS_AT, LENGTH)],
        ),
        sems,
    )
    values = hidden[...].astype(F32)
    packet[:LENGTH] = (values * gain[...].astype(F32)).astype(BF16)
    squares = jnp.sum(values * values, axis=1, keepdims=True)
    rows = jnp.concatenate([to_row(squares[:128]), to_row(squares[128:])], axis=0)
    high, low = two_terms(rows)
    packet[SQUARES_AT:COLUMNS_AT] = jnp.concatenate([high, low, jnp.zeros((12, 128), BF16)], axis=0)
    packet[COLUMNS_AT:GRADS_AT] = jnp.concatenate(
        [value_up[...], jnp.zeros((16, 128 - RANK), BF16)], axis=1
    )


def projection_kernel(place_ref, *rest):
    sources, out, held = rest[:4], rest[4], rest[5:9]
    q_levels, kv_levels, sems = rest[9:]
    half = pl.multiple_of(place_ref[0] * HALF, HALF)
    scales = pl.multiple_of(place_ref[0] * 128, 128)
    sources = (
        sources[0].at[pl.ds(half, HALF), :],
        sources[1].at[pl.ds(scales, 128), :],
        sources[2].at[:, pl.ds(half, HALF)],
        sources[3].at[:, pl.ds(scales, 128)],
    )
    fetch(sources, held, sems)
    wq, wq_scales, wkv, wkv_scales = held
    q_levels[...] = wq_scales[...].astype(F32)
    widen = lax.broadcasted_iota(jnp.int32, (32, 1024), 1) // 32 == lax.broadcasted_iota(
        jnp.int32, (32, 1024), 0
    )
    widen = jnp.where(widen, 1.0, 0.0).astype(BF16)
    for i in range(4):
        level = contract(wkv_scales[:, 32 * i : 32 * i + 32], widen, 1, 0)
        kv_levels[:, 1024 * i : 1024 * i + 1024] = level

    def step(j, carry):
        levels = q_levels[pl.ds(pl.multiple_of(j * 8, 8), 8), :]
        for e in range(2):
            rows = pl.ds(pl.multiple_of((2 * j + e) * 128, 128), 128)
            codes = wq[rows, :].astype(F32).reshape(4, 32, 128) * levels[4 * e : 4 * e + 4][:, None, :]
            out[rows, :] = codes.reshape(128, 128).astype(BF16)
            codes = wkv[:, rows].astype(F32) * kv_levels[:, rows]
            to = pl.multiple_of(HALF + (2 * j + e) * KV, KV)
            out[pl.ds(to, KV), :] = codes.astype(BF16)
        return carry

    lax.fori_loop(0, BLOCKS // 2, step, 0, unroll=2)


def output_kernel(place_ref, *rest):
    sources, out, (wo, wo_scales, sems) = rest[:2], rest[2], rest[3:]
    half = pl.ds(pl.multiple_of(place_ref[0] * HALF, HALF), HALF)
    fetch((sources[0].at[:, half], sources[1].at[:, half]), (wo, wo_scales), sems)

    def step(j, carry):
        block = pl.ds(pl.multiple_of(j * 128, 128), 128)
        level = wo_scales[:, block].astype(F32)
        codes = wo[:, block].astype(F32).reshape(4, 32, 128) * level[:, None, :]
        out[block, :] = codes.reshape(128, 128).astype(BF16)
        return carry

    lax.fori_loop(0, BLOCKS, step, 0, unroll=4)


def product_kernel(place_ref, gathered_at, *refs):
    weights, outputs, (kept, sent, box, value_up), gathered, sems = refs[:2], refs[2:4], refs[4:8], refs[8], refs[9]
    each = BLOCKS // PARTS
    copies = []
    for k in range(PARTS):
        part = pl.ds(k * each, each)
        copies.append(pltpu.make_async_copy(gathered_at.at[part], gathered.at[part], sems.at[k]))
        copies[-1].start()
    q = narrow = ctx = squares = 0.0
    for k in range(PARTS):
        copies[k].wait()
        blocks = range(k * each, (k + 1) * each)

        def rows(first, number, blocks=blocks):
            return jnp.concatenate([gathered[b, first : first + number, :] for b in blocks], axis=1)

        def block_rows(ref, first, number, blocks=blocks):
            return jnp.concatenate(
                [ref[first + b * number : first + (b + 1) * number, :] for b in blocks], axis=1
            )

        inputs = rows(0, LENGTH)
        span = slice(k * each * 128, (k + 1) * each * 128)
        q += contract(inputs, jnp.concatenate([w[span, :] for w in weights], axis=1), 1, 0)
        slim = [rows(DOWNS_AT, 2 * RANK)] + [block_rows(w, HALF, KV) for w in weights]
        narrow += contract(inputs, jnp.concatenate(slim, axis=0), 1, 1)
        wide = jnp.concatenate([block_rows(w, 0, 128) for w in outputs], axis=0)
        ctx += contract(rows(GRADS_AT, LENGTH), wide, 1, 1)
        for b in blocks:
            squares += gathered[b, SQUARES_AT : SQUARES_AT + 16, :].astype(F32)
    low, kv = narrow[:, : 2 * RANK], narrow[:, 2 * RANK :].T.astype(BF16)
    squares = squares[0:2] + squares[2:4]
    at_zero = place_ref[0] == 0
    for a in range(NX):
        mine = at_zero if a == 0 else jnp.logical_not(at_zero)
        whole = jnp.where(mine, kv[:KV], kv[KV:])
        whole = jnp.concatenate([whole[:, :128], whole[:, 128:]], axis=0)
        for i in range(GROUP):
            box[GROUP * a + i] = whole
    group = place_ref[1] // 4 * GROUP
    for i in range(GROUP):
        value_up[16 * i : 16 * i + 16, :] = gathered[group + i, COLUMNS_AT:GRADS_AT, :]
    high, rest = two_terms(squares)
    shared = jnp.concatenate([high.astype(F32), rest.astype(F32), jnp.zeros((12, 128), F32)], axis=0)
    for i, (out, cast) in enumerate(((kept, F32), (sent, BF16))):
        out[:LENGTH] = q[:, i * 128 : (i + 1) * 128].astype(cast)
        out[LENGTH:PER_HEAD] = ctx[:, i * 128 : (i + 1) * 128].astype(cast)
        out[PER_HEAD : PER_HEAD + LENGTH] = low.astype(cast)
        out[PER_HEAD + LENGTH :] = shared.astype(cast)


def turn(values, cosine, sine, axis):
    half = HEAD // 2
    if axis == 1:
        front, back = values[:, :half], values[:, half:]
    else:
        front, back = values[:half], values[half:]
    return jnp.concatenate([front * cosine - back * sine, back * cosine + front * sine], axis=axis)


def attention_kernel(
    kept,
    got,
    box,
    value_up_ref,
    hidden,
    gain,
    query_up,
    cosine,
    sine,
    cosine_t,
    sine_t,
    snapshot,
    out,
    up,
    normed,
):
    total = kept[...] + got[...].astype(F32)
    low = total[PER_HEAD : PER_HEAD + LENGTH]
    squares = total[PER_HEAD + LENGTH : PER_HEAD + LENGTH + 2]
    squares = squares + total[PER_HEAD + LENGTH + 2 : PER_HEAD + LENGTH + 4]
    inverse = lax.rsqrt(squares * (1.0 / FEATURES) + EPS)
    column = jnp.concatenate([to_column(inverse[0:1]), to_column(inverse[1:2])], axis=0)
    normed[...] = (hidden[...].astype(F32) * column * gain[...].astype(F32)).astype(BF16)
    lows = (low * column).astype(BF16)
    linear = total[:LENGTH] * column + ADAPTER_SCALE * contract(lows[:, :RANK], query_up[...], 1, 0)
    queries = turn(linear, cosine[...], sine[...], 1).astype(BF16)
    grads = total[LENGTH:PER_HEAD].astype(BF16)
    row_inverse = jnp.concatenate([inverse[0:1], inverse[1:2]], axis=1)
    value_up = value_up_ref[:, :RANK]

    def side(start):
        rows = []
        for i in range(start, start + GROUP // 2):
            part = sum(box[GROUP * a + i].astype(F32) for a in range(NX))
            rows.append(jnp.concatenate([part[:KV], part[KV:]], axis=1))
        return jnp.concatenate(rows, axis=0) * row_inverse

    keys = side(0).astype(BF16).astype(F32)
    keys = turn(keys, cosine_t[...], sine_t[...], 0).astype(BF16)
    values = (side(GROUP // 2) + ADAPTER_SCALE * contract(value_up, lows[:, RANK:], 1, 1)).astype(BF16)
    scale = HEAD ** (-0.5)
    scores = contract(queries, keys, 1, 0) * scale
    row = lax.broadcasted_iota(jnp.int32, (LENGTH, LENGTH), 0)
    column = lax.broadcasted_iota(jnp.int32, (LENGTH, LENGTH), 1)
    segment = snapshot[...].astype(F32)
    own = jnp.concatenate([to_column(segment[:, :128]), to_column(segment[:, 128:])], axis=0)
    allowed = jnp.logical_and(column <= row, own == segment)
    scores = jnp.where(allowed, scores, MASKED)
    weights = jnp.exp(scores - jnp.max(scores, axis=1, keepdims=True))
    prob = weights / jnp.sum(weights, axis=1, keepdims=True)
    grad_prob = contract(grads, values, 1, 0)
    grad_value = contract(prob.astype(BF16), grads, 0, 0).astype(BF16)
    inner = jnp.sum(prob * grad_prob, axis=1, keepdims=True)
    grad_score = (prob * (grad_prob - inner)).astype(BF16)
    grad_query = contract(grad_score, keys, 1, 1) * scale
    grad_linear = turn(grad_query, cosine[...], -sine[...], 1).astype(BF16)
    low_q, low_v = lows[:, :RANK], lows[:, RANK:]
    up[...] = ADAPTER_SCALE * contract(low_q, grad_linear, 0, 0)
    slices = ADAPTER_SCALE * contract(grad_value, low_v, 0, 0)
    slices = jnp.concatenate([slices, jnp.zeros((HEAD, 128 - RANK), F32)], axis=1).astype(BF16)
    grad_low = jnp.concatenate(
        [
            ADAPTER_SCALE * contract(grad_linear, query_up[...], 1, 1),
            ADAPTER_SCALE * contract(grad_value, value_up, 1, 0),
        ],
        axis=1,
    ).astype(BF16)
    rows = LENGTH // GROUP
    for i in range(GROUP):
        out[GROUP - 1 - i, :rows, :] = grad_low[i * rows : (i + 1) * rows]
        out[GROUP - 1 - i, rows:, :] = slices[16 * i : 16 * i + 16]


def near_kernel(parts, low, value):
    total = jnp.sum(parts[...].astype(F32), axis=0)
    rows = LENGTH // GROUP
    value[...] = total[rows:]
    for i in range(8):
        low[i] = total[:rows].astype(BF16)


def far_kernel(parts, low):
    total = jnp.sum(parts[...].astype(F32), axis=0).astype(BF16)
    for i in range(GROUP):
        low[i] = total


def rows_kernel(normed, low, up, value, out):
    whole = jnp.concatenate([low[GROUP - 1 - i] for i in range(GROUP)], axis=0)
    rows = contract(normed[...], whole, 0, 0).astype(BF16)
    last = jnp.concatenate([up[...], value[...]], axis=0).astype(BF16)
    for i in range(8):
        out[i, :HEAD, :] = rows
        out[i, HEAD:, :] = last


def total_kernel(parts, grad_a_query, query_up, grad_a_value, value):
    total = jnp.sum(parts[...].astype(F32), axis=0)
    rows = total[:HEAD].T
    grad_a_query[...] = rows[:RANK]
    grad_a_value[...] = rows[RANK:]
    query_up[...] = total[HEAD : HEAD + RANK]
    value[...] = total[HEAD + RANK :, :RANK]


def local(
    hidden_in,
    out_grad,
    snapshot_ids,
    norm_gain,
    wq_codes,
    wq_scales,
    wkv_codes,
    wkv_scales,
    wo_codes,
    wo_scales,
    a_query,
    query_up_weight,
    a_value,
    value_up_weight,
):
    head_index = lax.axis_index("fsdp")
    spot = jnp.stack([head_index // (NZ * NC), head_index // NC % NZ, head_index % NC]).astype(jnp.int32)
    gain = norm_gain[None, :]

    packet = call(
        pack_kernel,
        shape(PACKET, 128),
        hidden_in,
        gain,
        a_query,
        a_value,
        value_up_weight.T,
        out_grad,
        scratch=[
            pltpu.VMEM((LENGTH, 128), BF16),
            pltpu.VMEM((1, 128), BF16),
            pltpu.VMEM((16, RANK), BF16),
            pltpu.SemaphoreType.DMA((6,)),
        ],
        megabytes=56,
        held=True,
    )
    gathered = lax.all_gather(packet, "fsdp", axis=0, tiled=True, axis_index_groups=HALF_GROUPS)

    def projection(spot):
        return call(
            projection_kernel,
            shape(BLOCKS * (128 + KV), 128),
            spot,
            wq_codes,
            wq_scales,
            wkv_codes.T,
            wkv_scales.T,
            scratch=[
                pltpu.VMEM((HALF, 128), BF16),
                pltpu.VMEM((128, 128), BF16),
                pltpu.VMEM((KV, HALF), BF16),
                pltpu.VMEM((KV, 128), BF16),
                pltpu.VMEM((128, 128), F32),
                pltpu.VMEM((KV, HALF), F32),
                pltpu.SemaphoreType.DMA((4,)),
            ],
            megabytes=12,
            held=True,
        )

    def output(spot):
        return call(
            output_kernel,
            shape(BLOCKS * 128, 128),
            spot,
            wo_codes,
            wo_scales,
            scratch=[
                pltpu.VMEM((128, HALF), BF16),
                pltpu.VMEM((4, HALF), BF16),
                pltpu.SemaphoreType.DMA((2,)),
            ],
            megabytes=12,
            held=True,
        )

    other = spot ^ jnp.array([1, 0, 0], jnp.int32)
    sent_projection = projection(after(other, packet))
    sent_output = output(after(other, sent_projection))
    own_projection = projection(after(spot, sent_output))
    own_output = output(after(spot, own_projection))
    got_projection = swap_weights(sent_projection, NZ * NC)
    got_output = swap_weights(sent_output, NZ * NC)

    rows = PER_HEAD + SHARED
    gathered = gathered.reshape(BLOCKS, PACKET, 128)
    kept, sent, box, value_up = call(
        product_kernel,
        [
            shape(rows, 128, dtype=F32),
            shape(rows, 128),
            shape(2 * GROUP, 2 * KV, 128),
            shape(128, 128),
        ],
        spot,
        gathered,
        own_projection,
        got_projection,
        own_output,
        got_output,
        scratch=[
            pltpu.VMEM((BLOCKS, PACKET, 128), BF16),
            pltpu.SemaphoreType.DMA((PARTS,)),
        ],
        megabytes=50,
        held=(1,),
    )
    got = swap(sent, NZ * NC)
    box = exchange(box, "fsdp", BOX_GROUPS)

    cosine, sine = rope_tables()
    slices, up, normed = call(
        attention_kernel,
        [shape(GROUP, LENGTH // GROUP + 16, 128), shape(RANK, HEAD, dtype=F32), shape(LENGTH, 128)],
        kept,
        got,
        box,
        value_up,
        hidden_in,
        gain,
        query_up_weight,
        jnp.asarray(cosine),
        jnp.asarray(sine),
        jnp.asarray(cosine.T.copy()),
        jnp.asarray(sine.T.copy()),
        snapshot_ids,
    )

    low, value = call(
        near_kernel,
        [shape(8, LENGTH // GROUP, 128), shape(16, 128, dtype=F32)],
        exchange(slices, "fsdp", NEAR_GROUPS),
    )
    low = call(far_kernel, shape(GROUP, LENGTH // GROUP, 128), exchange(low, "fsdp", FAR_GROUPS))
    mine = call(
        rows_kernel,
        shape(8, HEAD + RANK + 16, 128),
        normed,
        exchange(low, "fsdp", NEAR_GROUPS),
        up,
        value,
    )
    grad_a_query, query_up, grad_a_value, value = call(
        total_kernel,
        [
            shape(RANK, HEAD, dtype=F32),
            shape(RANK, HEAD, dtype=F32),
            shape(RANK, HEAD, dtype=F32),
            shape(16, RANK, dtype=F32),
        ],
        exchange(mine, "dp", [list(range(7, -1, -1))]),
    )
    return grad_a_query.T, query_up, grad_a_value.T, value.T


def solution(mesh):
    in_specs = (
        P("dp", "fsdp"),
        P("dp", "fsdp"),
        P("dp", None),
        P("fsdp"),
        P(None, "fsdp"),
        P(None, "fsdp"),
        P(None, "fsdp"),
        P(None, "fsdp"),
        P("fsdp", None),
        P("fsdp", None),
        P(None, "fsdp"),
        P(None, "fsdp"),
        P(None, "fsdp"),
        P(None, "fsdp"),
    )
    out_specs = (P("fsdp", None), P(None, "fsdp"), P("fsdp", None), P(None, "fsdp"))
    return jax.shard_map(local, mesh=mesh, in_specs=in_specs, out_specs=out_specs, check_vma=False)
```

```python
import math

import jax
import jax.numpy as jnp
import numpy as np
from jax import lax
from jax.experimental import pallas as pl
from jax.experimental.pallas import tpu as pltpu
from jax.sharding import PartitionSpec as P

GROUP = 8
EPS = 1e-05
ADAPTER_SCALE = 0.5
ROPE_BASE = 500000.0
MASKED = -1e30

NX, NZ, NC = 2, 16, 2
LENGTH, HEAD, RANK, KV = 256, 128, 64, 32
FEATURES = NX * NZ * NC * HEAD
HALF = FEATURES // NX
PARTS = 8
BLOCKS = NZ * NC
DOWNS_AT = LENGTH
COLUMNS_AT = DOWNS_AT + 2 * RANK
GRADS_AT = COLUMNS_AT + 16
PACKET = GRADS_AT + LENGTH
PER_HEAD = 2 * LENGTH
SHARED = LENGTH + 16

F32, BF16 = jnp.float32, jnp.bfloat16
VMEM = pl.BlockSpec(memory_space=pltpu.VMEM)
SMEM = pl.BlockSpec(memory_space=pltpu.SMEM)


def place(a, z, c):
    return a * (NZ * NC) + z * NC + c


HALF_GROUPS = [[place(a, z, c) for z in range(NZ) for c in range(NC)] for a in range(NX)]
BOX_GROUPS = [
    [place(a, 4 * b + i, c) for a in range(NX) for i in range(4) for c in range(NC)] for b in range(4)
]
NEAR_GROUPS = [[GROUP * g + i for i in range(GROUP)][::-1] for g in range(8)]
FAR_GROUPS = [
    [place(a, z + 4 * k, c) for a in range(NX) for k in (2, 3, 0, 1)] for z in range(4) for c in range(NC)
]


def swap(value, mask):
    return lax.ppermute(value, "fsdp", [(i, i ^ mask) for i in range(NX * NZ * NC)])


def swap_weights(value, mask):
    if mask < NZ * NC:
        return swap(value, mask)
    size = NX * NZ * NC
    rows = lax.axis_size("dp")
    pairs = [(d * size + i, (d ^ 1) * size + (i ^ mask)) for d in range(rows) for i in range(size)]
    return lax.ppermute(value, ("dp", "fsdp"), pairs)


def exchange(value, axis, groups=None):
    return lax.all_to_all(value, axis, 0, 0, axis_index_groups=groups)


def after(value, *others):
    return lax.optimization_barrier((value, *others))[0]


def rope_tables():
    positions = np.arange(LENGTH, dtype=np.float32)[:, None]
    steps = np.arange(HEAD // 2, dtype=np.float32)
    frequency = np.exp(steps * np.float32(-2.0 * math.log(ROPE_BASE) / HEAD)).astype(np.float32)
    angles = positions * frequency[None, :]
    return np.cos(angles).astype(np.float32), np.sin(angles).astype(np.float32)


def contract(left_arr, right_arr, left_dim, right_dim):
    return lax.dot_general(
        left_arr,
        right_arr,
        (((left_dim,), (right_dim,)), ((), ())),
        preferred_element_type=F32,
    )


def two_terms(value):
    high = value.astype(BF16)
    return high, (value - high.astype(F32)).astype(BF16)


def call(body, outs, *operands, scratch=(), megabytes=32, held=False):
    specs = [SMEM if o.dtype == jnp.int32 and o.ndim == 1 else VMEM for o in operands]
    if held is not False:
        here = range(len(operands)) if held is True else held
        specs = [
            pl.BlockSpec(memory_space=pl.ANY) if i in here and spec is not SMEM else spec
            for i, spec in enumerate(specs)
        ]
    many = isinstance(outs, (list, tuple))
    return pl.pallas_call(
        body,
        out_shape=outs,
        in_specs=specs,
        out_specs=[VMEM] * len(outs) if many else VMEM,
        scratch_shapes=list(scratch),
        compiler_params=pltpu.CompilerParams(vmem_limit_bytes=megabytes << 20),
    )(*operands)


def shape(*dims, dtype=BF16):
    return jax.ShapeDtypeStruct(dims, dtype)


def diagonal(size):
    return lax.broadcasted_iota(jnp.int32, (size, size), 0) == lax.broadcasted_iota(
        jnp.int32, (size, size), 1
    )


def to_row(column):
    return jnp.sum(jnp.where(diagonal(128), column, 0.0), axis=0, keepdims=True)


def to_column(row):
    return jnp.sum(jnp.where(diagonal(128), row, 0.0), axis=1, keepdims=True)


def fetch(sources, targets, sems):
    copies = [pltpu.make_async_copy(a, b, sems.at[i]) for i, (a, b) in enumerate(zip(sources, targets))]
    for copy in copies:
        copy.start()
    for copy in copies:
        copy.wait()


def pack_kernel(
    hidden_at, gain_at, a_query_at, a_value_at, value_up_at, grad_at, packet, hidden, gain, value_up, sems
):
    fetch(
        (hidden_at, gain_at, value_up_at, a_query_at, a_value_at, grad_at),
        (
            hidden,
            gain,
            value_up,
            packet.at[pl.ds(DOWNS_AT, RANK)],
            packet.at[pl.ds(DOWNS_AT + RANK, RANK)],
            packet.at[pl.ds(GRADS_AT, LENGTH)],
        ),
        sems,
    )
    values = hidden[...].astype(F32)
    packet[:LENGTH] = (values * gain[...].astype(F32)).astype(BF16)
    squares = jnp.sum(values * values, axis=1, keepdims=True)
    rows = jnp.concatenate([to_row(squares[:128]), to_row(squares[128:])], axis=0)
    high, low = two_terms(rows)
    right = [high[:, :RANK], high[:, RANK:], low[:, :RANK], low[:, RANK:], jnp.zeros((8, 128 - RANK), BF16)]
    packet[COLUMNS_AT:GRADS_AT] = jnp.concatenate(
        [value_up[...], jnp.concatenate(right, axis=0)], axis=1
    )


def projection_kernel(place_ref, *rest):
    sources, out, held = rest[:4], rest[4], rest[5:9]
    q_levels, kv_levels, sems = rest[9:]
    half = pl.multiple_of(place_ref[0] * HALF, HALF)
    scales = pl.multiple_of(place_ref[0] * 128, 128)
    sources = (
        sources[0].at[pl.ds(half, HALF), :],
        sources[1].at[pl.ds(scales, 128), :],
        sources[2].at[:, pl.ds(half, HALF)],
        sources[3].at[:, pl.ds(scales, 128)],
    )
    fetch(sources, held, sems)
    wq, wq_scales, wkv, wkv_scales = held
    q_levels[...] = wq_scales[...].astype(F32)
    widen = lax.broadcasted_iota(jnp.int32, (32, 1024), 1) // 32 == lax.broadcasted_iota(
        jnp.int32, (32, 1024), 0
    )
    widen = jnp.where(widen, 1.0, 0.0).astype(BF16)
    for i in range(4):
        level = contract(wkv_scales[:, 32 * i : 32 * i + 32], widen, 1, 0)
        kv_levels[:, 1024 * i : 1024 * i + 1024] = level

    def step(j, carry):
        levels = q_levels[pl.ds(pl.multiple_of(j * 8, 8), 8), :]
        for e in range(2):
            rows = pl.ds(pl.multiple_of((2 * j + e) * 128, 128), 128)
            codes = wq[rows, :].astype(F32).reshape(4, 32, 128) * levels[4 * e : 4 * e + 4][:, None, :]
            out[rows, :] = codes.reshape(128, 128).astype(BF16)
            codes = wkv[:, rows].astype(F32) * kv_levels[:, rows]
            to = pl.multiple_of(HALF + (2 * j + e) * KV, KV)
            out[pl.ds(to, KV), :] = codes.astype(BF16)
        return carry

    lax.fori_loop(0, BLOCKS // 2, step, 0, unroll=2)


def output_kernel(place_ref, *rest):
    sources, out, (wo, wo_scales, sems) = rest[:2], rest[2], rest[3:]
    half = pl.ds(pl.multiple_of(place_ref[0] * HALF, HALF), HALF)
    fetch((sources[0].at[:, half], sources[1].at[:, half]), (wo, wo_scales), sems)

    def step(j, carry):
        block = pl.ds(pl.multiple_of(j * 128, 128), 128)
        level = wo_scales[:, block].astype(F32)
        codes = wo[:, block].astype(F32).reshape(4, 32, 128) * level[:, None, :]
        out[block, :] = codes.reshape(128, 128).astype(BF16)
        return carry

    lax.fori_loop(0, BLOCKS, step, 0, unroll=4)


def product_kernel(place_ref, gathered_at, *refs):
    weights, outputs, (kept, sent, box, value_up), gathered, sems = refs[:2], refs[2:4], refs[4:8], refs[8], refs[9]
    each = BLOCKS // PARTS
    copies = []
    for k in range(PARTS):
        part = pl.ds(k * each, each)
        copies.append(pltpu.make_async_copy(gathered_at.at[part], gathered.at[part], sems.at[k]))
        copies[-1].start()
    q = narrow = ctx = squares = 0.0
    for k in range(PARTS):
        copies[k].wait()
        blocks = range(k * each, (k + 1) * each)

        def rows(first, number, blocks=blocks):
            return jnp.concatenate([gathered[b, first : first + number, :] for b in blocks], axis=1)

        def block_rows(ref, first, number, blocks=blocks):
            return jnp.concatenate(
                [ref[first + b * number : first + (b + 1) * number, :] for b in blocks], axis=1
            )

        inputs = rows(0, LENGTH)
        span = slice(k * each * 128, (k + 1) * each * 128)
        q += contract(inputs, jnp.concatenate([w[span, :] for w in weights], axis=1), 1, 0)
        slim = [rows(DOWNS_AT, 2 * RANK)] + [block_rows(w, HALF, KV) for w in weights]
        narrow += contract(inputs, jnp.concatenate(slim, axis=0), 1, 1)
        wide = jnp.concatenate([block_rows(w, 0, 128) for w in outputs], axis=0)
        ctx += contract(rows(GRADS_AT, LENGTH), wide, 1, 1)
        for b in blocks:
            squares += gathered[b, COLUMNS_AT:GRADS_AT, :].astype(F32)
    low, kv = narrow[:, : 2 * RANK], narrow[:, 2 * RANK :].T.astype(BF16)
    squares = squares[:4, RANK:] + squares[4:8, RANK:]
    squares = jnp.concatenate([squares[0:2], squares[2:4]], axis=1)
    at_zero = place_ref[0] == 0
    for a in range(NX):
        mine = at_zero if a == 0 else jnp.logical_not(at_zero)
        whole = jnp.where(mine, kv[:KV], kv[KV:])
        whole = jnp.concatenate([whole[:, :128], whole[:, 128:]], axis=0)
        for i in range(GROUP):
            box[GROUP * a + i] = whole
    group = place_ref[1] // 4 * GROUP
    for i in range(GROUP):
        value_up[16 * i : 16 * i + 16, :] = gathered[group + i, COLUMNS_AT:GRADS_AT, :]
    high, rest = two_terms(squares)
    shared = jnp.concatenate([high.astype(F32), rest.astype(F32), jnp.zeros((12, 128), F32)], axis=0)
    for i, (out, cast) in enumerate(((kept, F32), (sent, BF16))):
        out[:LENGTH] = q[:, i * 128 : (i + 1) * 128].astype(cast)
        out[LENGTH:PER_HEAD] = ctx[:, i * 128 : (i + 1) * 128].astype(cast)
        out[PER_HEAD : PER_HEAD + LENGTH] = low.astype(cast)
        out[PER_HEAD + LENGTH :] = shared.astype(cast)


def turn(values, cosine, sine, axis):
    half = HEAD // 2
    if axis == 1:
        front, back = values[:, :half], values[:, half:]
    else:
        front, back = values[:half], values[half:]
    return jnp.concatenate([front * cosine - back * sine, back * cosine + front * sine], axis=axis)


def attention_kernel(
    kept,
    got,
    box,
    value_up_ref,
    hidden,
    gain,
    query_up,
    cosine,
    sine,
    cosine_t,
    sine_t,
    snapshot,
    out,
    up,
    normed,
):
    total = kept[...] + got[...].astype(F32)
    low = total[PER_HEAD : PER_HEAD + LENGTH]
    squares = total[PER_HEAD + LENGTH : PER_HEAD + LENGTH + 2]
    squares = squares + total[PER_HEAD + LENGTH + 2 : PER_HEAD + LENGTH + 4]
    inverse = lax.rsqrt(squares * (1.0 / FEATURES) + EPS)
    column = jnp.concatenate([to_column(inverse[0:1]), to_column(inverse[1:2])], axis=0)
    normed[...] = (hidden[...].astype(F32) * column * gain[...].astype(F32)).astype(BF16)
    lows = (low * column).astype(BF16)
    linear = total[:LENGTH] * column + ADAPTER_SCALE * contract(lows[:, :RANK], query_up[...], 1, 0)
    queries = turn(linear, cosine[...], sine[...], 1).astype(BF16)
    grads = total[LENGTH:PER_HEAD].astype(BF16)
    row_inverse = jnp.concatenate([inverse[0:1], inverse[1:2]], axis=1)
    value_up = value_up_ref[:, :RANK]

    def side(start):
        rows = []
        for i in range(start, start + GROUP // 2):
            part = sum(box[GROUP * a + i].astype(F32) for a in range(NX))
            rows.append(jnp.concatenate([part[:KV], part[KV:]], axis=1))
        return jnp.concatenate(rows, axis=0) * row_inverse

    keys = side(0).astype(BF16).astype(F32)
    keys = turn(keys, cosine_t[...], sine_t[...], 0).astype(BF16)
    values = (side(GROUP // 2) + ADAPTER_SCALE * contract(value_up, lows[:, RANK:], 1, 1)).astype(BF16)
    scale = HEAD ** (-0.5)
    scores = contract(queries, keys, 1, 0) * scale
    row = lax.broadcasted_iota(jnp.int32, (LENGTH, LENGTH), 0)
    column = lax.broadcasted_iota(jnp.int32, (LENGTH, LENGTH), 1)
    segment = snapshot[...].astype(F32)
    own = jnp.concatenate([to_column(segment[:, :128]), to_column(segment[:, 128:])], axis=0)
    allowed = jnp.logical_and(column <= row, own == segment)
    scores = jnp.where(allowed, scores, MASKED)
    weights = jnp.exp(scores - jnp.max(scores, axis=1, keepdims=True))
    prob = weights / jnp.sum(weights, axis=1, keepdims=True)
    grad_prob = contract(grads, values, 1, 0)
    grad_value = contract(prob.astype(BF16), grads, 0, 0).astype(BF16)
    inner = jnp.sum(prob * grad_prob, axis=1, keepdims=True)
    grad_score = (prob * (grad_prob - inner)).astype(BF16)
    grad_query = contract(grad_score, keys, 1, 1) * scale
    grad_linear = turn(grad_query, cosine[...], -sine[...], 1).astype(BF16)
    low_q, low_v = lows[:, :RANK], lows[:, RANK:]
    up[...] = ADAPTER_SCALE * contract(low_q, grad_linear, 0, 0)
    slices = ADAPTER_SCALE * contract(grad_value, low_v, 0, 0)
    slices = jnp.concatenate([slices, jnp.zeros((HEAD, 128 - RANK), F32)], axis=1).astype(BF16)
    grad_low = jnp.concatenate(
        [
            ADAPTER_SCALE * contract(grad_linear, query_up[...], 1, 1),
            ADAPTER_SCALE * contract(grad_value, value_up, 1, 0),
        ],
        axis=1,
    ).astype(BF16)
    rows = LENGTH // GROUP
    for i in range(GROUP):
        out[GROUP - 1 - i, :rows, :] = grad_low[i * rows : (i + 1) * rows]
        out[GROUP - 1 - i, rows:, :] = slices[16 * i : 16 * i + 16]


def near_kernel(parts, low, value):
    total = jnp.sum(parts[...].astype(F32), axis=0)
    rows = LENGTH // GROUP
    value[...] = total[rows:]
    for i in range(8):
        low[i] = total[:rows].astype(BF16)


def far_kernel(parts, low):
    total = jnp.sum(parts[...].astype(F32), axis=0).astype(BF16)
    for i in range(GROUP):
        low[i] = total


def rows_kernel(normed, low, up, value, out):
    whole = jnp.concatenate([low[GROUP - 1 - i] for i in range(GROUP)], axis=0)
    rows = contract(normed[...], whole, 0, 0).astype(BF16)
    last = jnp.concatenate([up[...], value[...]], axis=0).astype(BF16)
    for i in range(8):
        out[i, :HEAD, :] = rows
        out[i, HEAD:, :] = last


def total_kernel(parts, grad_a_query, query_up, grad_a_value, value):
    total = jnp.sum(parts[...].astype(F32), axis=0)
    rows = total[:HEAD].T
    grad_a_query[...] = rows[:RANK]
    grad_a_value[...] = rows[RANK:]
    query_up[...] = total[HEAD : HEAD + RANK]
    value[...] = total[HEAD + RANK :, :RANK]


def local(
    hidden_in,
    out_grad,
    snapshot_ids,
    norm_gain,
    wq_codes,
    wq_scales,
    wkv_codes,
    wkv_scales,
    wo_codes,
    wo_scales,
    a_query,
    query_up_weight,
    a_value,
    value_up_weight,
):
    head_index = lax.axis_index("fsdp")
    spot = jnp.stack([head_index // (NZ * NC), head_index // NC % NZ, head_index % NC]).astype(jnp.int32)
    gain = norm_gain[None, :]

    packet = call(
        pack_kernel,
        shape(PACKET, 128),
        hidden_in,
        gain,
        a_query,
        a_value,
        value_up_weight.T,
        out_grad,
        scratch=[
            pltpu.VMEM((LENGTH, 128), BF16),
            pltpu.VMEM((1, 128), BF16),
            pltpu.VMEM((16, RANK), BF16),
            pltpu.SemaphoreType.DMA((6,)),
        ],
        megabytes=56,
        held=True,
    )
    gathered = lax.all_gather(packet, "fsdp", axis=0, tiled=True, axis_index_groups=HALF_GROUPS)

    def projection(spot):
        return call(
            projection_kernel,
            shape(BLOCKS * (128 + KV), 128),
            spot,
            wq_codes,
            wq_scales,
            wkv_codes.T,
            wkv_scales.T,
            scratch=[
                pltpu.VMEM((HALF, 128), BF16),
                pltpu.VMEM((128, 128), BF16),
                pltpu.VMEM((KV, HALF), BF16),
                pltpu.VMEM((KV, 128), BF16),
                pltpu.VMEM((128, 128), F32),
                pltpu.VMEM((KV, HALF), F32),
                pltpu.SemaphoreType.DMA((4,)),
            ],
            megabytes=12,
            held=True,
        )

    def output(spot):
        return call(
            output_kernel,
            shape(BLOCKS * 128, 128),
            spot,
            wo_codes,
            wo_scales,
            scratch=[
                pltpu.VMEM((128, HALF), BF16),
                pltpu.VMEM((4, HALF), BF16),
                pltpu.SemaphoreType.DMA((2,)),
            ],
            megabytes=12,
            held=True,
        )

    other = spot ^ jnp.array([1, 0, 0], jnp.int32)
    sent_projection = projection(after(other, packet))
    sent_output = output(after(other, sent_projection))
    own_projection = projection(after(spot, sent_output))
    own_output = output(after(spot, own_projection))
    got_projection = swap_weights(sent_projection, NZ * NC)
    got_output = swap_weights(sent_output, NZ * NC)

    rows = PER_HEAD + SHARED
    gathered = gathered.reshape(BLOCKS, PACKET, 128)
    kept, sent, box, value_up = call(
        product_kernel,
        [
            shape(rows, 128, dtype=F32),
            shape(rows, 128),
            shape(2 * GROUP, 2 * KV, 128),
            shape(128, 128),
        ],
        spot,
        gathered,
        own_projection,
        got_projection,
        own_output,
        got_output,
        scratch=[
            pltpu.VMEM((BLOCKS, PACKET, 128), BF16),
            pltpu.SemaphoreType.DMA((PARTS,)),
        ],
        megabytes=50,
        held=(1,),
    )
    got = swap(sent, NZ * NC)
    box = exchange(box, "fsdp", BOX_GROUPS)

    cosine, sine = rope_tables()
    slices, up, normed = call(
        attention_kernel,
        [shape(GROUP, LENGTH // GROUP + 16, 128), shape(RANK, HEAD, dtype=F32), shape(LENGTH, 128)],
        kept,
        got,
        box,
        value_up,
        hidden_in,
        gain,
        query_up_weight,
        jnp.asarray(cosine),
        jnp.asarray(sine),
        jnp.asarray(cosine.T.copy()),
        jnp.asarray(sine.T.copy()),
        snapshot_ids,
    )

    low, value = call(
        near_kernel,
        [shape(8, LENGTH // GROUP, 128), shape(16, 128, dtype=F32)],
        exchange(slices, "fsdp", NEAR_GROUPS),
    )
    low = call(far_kernel, shape(GROUP, LENGTH // GROUP, 128), exchange(low, "fsdp", FAR_GROUPS))
    mine = call(
        rows_kernel,
        shape(8, HEAD + RANK + 16, 128),
        normed,
        exchange(low, "fsdp", NEAR_GROUPS),
        up,
        value,
    )
    grad_a_query, query_up, grad_a_value, value = call(
        total_kernel,
        [
            shape(RANK, HEAD, dtype=F32),
            shape(RANK, HEAD, dtype=F32),
            shape(RANK, HEAD, dtype=F32),
            shape(16, RANK, dtype=F32),
        ],
        exchange(mine, "dp", [list(range(7, -1, -1))]),
    )
    return grad_a_query.T, query_up, grad_a_value.T, value.T


def solution(mesh):
    in_specs = (
        P("dp", "fsdp"),
        P("dp", "fsdp"),
        P("dp", None),
        P("fsdp"),
        P(None, "fsdp"),
        P(None, "fsdp"),
        P(None, "fsdp"),
        P(None, "fsdp"),
        P("fsdp", None),
        P("fsdp", None),
        P(None, "fsdp"),
        P(None, "fsdp"),
        P(None, "fsdp"),
        P(None, "fsdp"),
    )
    out_specs = (P("fsdp", None), P(None, "fsdp"), P("fsdp", None), P(None, "fsdp"))
    return jax.shard_map(local, mesh=mesh, in_specs=in_specs, out_specs=out_specs, check_vma=False)
```
